128 devices in a mesh: ctx: 16 (over x, y), head: 8 (over z, core).
Axes of the slice: x: 4, y: 4, z: 4, core: 2. Of those that a mesh axis runs over, the one named last changes fastest.
Arguments:
- tokens: bfloat16 [65536, 2048], P(('ctx', 'head')), may hold values from -6 to 6
- picks: int32 [16384], P(('ctx', 'head')), may hold values from 0 to 511, as said below
- counts: int32 [128], P(('ctx', 'head')), may hold values from 1 to 128, 8192 in all
- score: float32 [16384], P(('ctx', 'head')), may hold values from 0.25 to 1
- w_in: bfloat16 [2048, 8192], P(None, 'head'), may hold values from -0.125 to 0.125
- w_out: bfloat16 [8192, 2048], P('head'), may hold values from -0.0625 to 0.0625
- cotan: bfloat16 [16384, 2048], P(('ctx', 'head')), may hold values from -6 to 6
Outputs:
- heavy: bfloat16 [16384, 2048], P(('ctx', 'head'))
- grad_x: bfloat16 [65536, 2048], P(('ctx', 'head'))
- grad_score: float32 [16384], P(('ctx', 'head'))
- grad_in: float32 [2048, 8192], P('ctx', 'head')
- grad_out: float32 [8192, 2048], P('head', 'ctx')
The draws below stay inside these ranges and needn't reach their ends.
Inputs may be any that keep to these rules, and one draw needn't show every extreme that they name: `picks`: the 128 entries of one device are distinct positions of that device's 512 tokens.
All inputs are finite; a program needn't handle non-finite values. No bound on the sum of `counts` on one device may be relied on, other than what follows from the above.
Results may differ from the reference program's by a relative error of at most 0.027.
Values may be sent and summed in bfloat16 or wider, within the bound.
No kernel may reach another device: no remote copies, remote signals or barrier semaphores. Data moves between devices by JAX's collectives and lax.ppermute only.
A program may use at most 128 MiB of HBM per device.

```python
import math
import jax
import jax.numpy as jnp
import numpy as np
from jax import lax

D = 2048
FF = 8192
TOK_DEV = 512
ROUTED = 128
TOKENS = 65536
ROWS = 16384
N_CTX = 16
N_HEAD = 8


def draw_picks(key, part):
    key = jax.random.fold_in(key, 11)
    keys = jax.random.split(key, ROWS // ROUTED)
    lists = jax.vmap(lambda k: jax.random.permutation(k, TOK_DEV)[:ROUTED])(keys)
    return lists.reshape(ROWS).astype(jnp.int32)


def level_of(rng, dims, cuts, smallest, top_value):
    def one(position, shards_of):
        draws = jax.random.uniform(jax.random.fold_in(jax.random.fold_in(rng, 6), position), (shards_of,), jnp.float32, smallest / len(cuts), top_value / len(cuts))
        return jnp.repeat(jnp.exp(draws), dims[position] // shards_of).reshape((-1,) + (1,) * (len(dims) - position - 1))

    factor_of = one(*cuts[0])
    for cut in cuts[1:]:
        factor_of = factor_of * one(*cut)
    return factor_of


def length_profile(amount, total, reach, skew):
    loads = [(1 << 20) // math.isqrt(rank ** skew) + 1 for rank in range(2, amount + 1)]
    spare, given = total - reach - (amount - 1), [1] * (amount - 1)
    while spare > 0:
        candidates = [i for i in range(amount - 1) if given[i] < reach]
        pool, budget = sum([loads[i] for i in candidates]), spare
        for i in candidates:
            addition = min(reach - given[i], max(1, budget * loads[i] // pool), spare)
            given[i] = given[i] + addition
            spare = spare - addition
    return np.array([reach] + given)


def uneven(rng, count, total, reach, skew):
    if count == 2:
        one = jax.random.randint(rng, (), max(1, total - reach), min(reach, total - 1) + 1)
        return jnp.stack([one, total - one])
    lengths = jnp.asarray(length_profile(count, total, reach, skew), jnp.int32)
    pairs = (count - 1) // 2
    giver, sink = lengths[1:1 + 2 * pairs:2], lengths[2:2 + 2 * pairs:2]
    slack = jnp.minimum(giver - 1, reach - sink)
    moved = jax.random.randint(jax.random.fold_in(rng, 1), (pairs,), 0, 1 << 20) % (slack + 1)
    lengths = lengths.at[1:1 + 2 * pairs:2].set(giver - moved).at[2:2 + 2 * pairs:2].set(sink + moved)
    return lengths[jax.random.permutation(jax.random.fold_in(rng, 2), count)]


def noise(own_key, extent, scale, most, shards=(), held_as=jnp.bfloat16):
    factor_of = level_of(own_key, extent, shards, -0.22, 0.18) if shards else 1.0
    drawn = jax.random.normal(own_key, extent, jnp.float32) * scale * factor_of
    return jnp.minimum(jnp.maximum(drawn, -most), most).astype(held_as)


def setup_inputs(seed: int = 0) -> dict:
    key_of = jax.random.split(jax.random.key(seed), 8)
    return {
        "tokens": noise(key_of[0], (TOKENS, D), 1.0, 6.0, ((0, 128),)),
        "picks": draw_picks(jax.random.fold_in(key_of[7], 71), 0),
        "counts": uneven(key_of[2], N_CTX * N_HEAD, N_CTX * N_HEAD * ROUTED // 2, ROUTED, 2).astype(jnp.int32),
        "score": jnp.clip(jnp.exp(math.log(1.0) - 1.3862944 * jax.random.uniform(key_of[3], (ROWS,), jnp.float32) ** level_of(key_of[3], (ROWS,), ((0, 128),), -0.2, 0.2)), 0.25, 1.0),
        "w_in": noise(key_of[4], (D, FF), D ** -0.5, 0.125, ((1, 8),)),
        "w_out": noise(key_of[5], (FF, D), FF ** -0.5, 0.0625, ((0, 8),)),
        "cotan": noise(key_of[6], (ROWS, D), 1.0, 6.0, ((0, 128),)),
    }


def gelu_parts(u):
    c = 0.7978845608
    t = jnp.tanh(c * (u + 0.044715 * u * u * u))
    value = 0.5 * u * (1.0 + t)
    slope = 0.5 * (1.0 + t) + 0.5 * u * (1.0 - t * t) * c * (1.0 + 3.0 * 0.044715 * u * u)
    return value, slope


def reference(tokens, picks, counts, score, w_in, w_out, cotan):
    slots = jnp.arange(ROWS, dtype=jnp.int32)
    device = slots // ROUTED
    live = (slots % ROUTED) < counts[device]
    place = (picks + device * TOK_DEV).astype(jnp.int32)
    rows = jnp.where(live[:, None], tokens[place], jnp.zeros((), jnp.bfloat16)).astype(jnp.bfloat16)
    dffn = (score[:, None] * cotan.astype(jnp.float32) * live[:, None].astype(jnp.float32)).astype(jnp.bfloat16)
    pre = jnp.dot(rows, w_in, preferred_element_type=jnp.float32)
    value, slope = gelu_parts(pre)
    hidden = value.astype(jnp.bfloat16)
    group = FF // N_HEAD
    ffn_sum = jnp.zeros((ROWS, D), jnp.float32)
    for g in range(N_HEAD):
        part = jnp.dot(hidden[:, g * group:(g + 1) * group], w_out[g * group:(g + 1) * group, :], preferred_element_type=jnp.float32)
        ffn_sum = ffn_sum + part.astype(jnp.bfloat16).astype(jnp.float32)
    ffn = lax.optimization_barrier(ffn_sum.astype(jnp.bfloat16)).astype(jnp.float32)
    heavy = (score[:, None] * ffn).astype(jnp.bfloat16)
    grad_score = jnp.sum(cotan.astype(jnp.float32) * ffn, axis=1)
    dhid = lax.dot_general(dffn, w_out, (((1,), (1,)), ((), ())), preferred_element_type=jnp.float32)
    dpre = (dhid * slope).astype(jnp.bfloat16)
    grad_out = lax.dot_general(hidden, dffn, (((0,), (0,)), ((), ())), preferred_element_type=jnp.float32)
    grad_in = lax.dot_general(rows, dpre, (((0,), (0,)), ((), ())), preferred_element_type=jnp.float32)
    dx_sum = jnp.zeros((ROWS, D), jnp.float32)
    for g in range(N_HEAD):
        part = lax.dot_general(dpre[:, g * group:(g + 1) * group], w_in[:, g * group:(g + 1) * group], (((1,), (1,)), ((), ())), preferred_element_type=jnp.float32)
        dx_sum = dx_sum + part.astype(jnp.bfloat16).astype(jnp.float32)
    dxr = dx_sum.astype(jnp.bfloat16)
    grad_x = jnp.zeros((TOKENS, D), jnp.bfloat16).at[place].set(dxr)
    return heavy, grad_x, grad_score, grad_in, grad_out
```

```python
import jax
import jax.numpy as jnp
from jax import lax
from jax.sharding import PartitionSpec as P

F32 = jnp.float32
BF16 = jnp.bfloat16
SIDE = 4


def gelu_parts(u):
    c = 0.7978845608
    t = jnp.tanh(c * (u + 0.044715 * u * u * u))
    value = 0.5 * u * (1.0 + t)
    slope = 0.5 * (1.0 + t) + 0.5 * u * (1.0 - t * t) * c * (1.0 + 3.0 * 0.044715 * u * u)
    return (value, slope)


def move_x(v, by):
    perm = [(x * SIDE + y, ((x + by) % SIDE) * SIDE + y) for x in range(SIDE) for y in range(SIDE)]
    return lax.ppermute(v, "ctx", perm)


def move_y(v, by):
    perm = [(x * SIDE + y, x * SIDE + (y + by) % SIDE) for x in range(SIDE) for y in range(SIDE)]
    return lax.ppermute(v, "ctx", perm)


def move_z(v, by):
    perm = [(z * 2 + c, ((z + by) % SIDE) * 2 + c) for z in range(SIDE) for c in range(2)]
    return lax.ppermute(v, "head", perm)


def swap_core(v):
    return lax.ppermute(v, "head", [(i, i ^ 1) for i in range(2 * SIDE)])


def dot(a, b, dims):
    return lax.dot_general(a, b, ((dims[0], dims[1]), ((), ())), preferred_element_type=F32)


def ring_scatter(make, move):
    far0, far1 = make(2, 0).astype(BF16), make(2, 1).astype(BF16)
    up1, down0 = make(1, 1).astype(BF16), make(-1, 0).astype(BF16)
    from_below = move(jnp.stack([far0, up1]), 1)
    from_above = move(jnp.stack([far1, down0]), -1)
    up0 = (make(1, 0) + from_below[0].astype(F32)).astype(BF16)
    down1 = (make(-1, 1) + from_above[0].astype(F32)).astype(BF16)
    below0 = move(up0, 1)
    above1 = move(down1, -1)
    half0 = make(0, 0) + below0.astype(F32) + from_above[1].astype(F32)
    half1 = make(0, 1) + from_below[1].astype(F32) + above1.astype(F32)
    return half0, half1


def direct_scatter(cut, move):
    terms = [move(cut(k).astype(BF16), k).astype(F32) for k in (1, -1, 2)]
    return cut(0).astype(F32) + terms[0] + terms[1] + terms[2]


def on_device(tokens, picks, counts, score, w_in, w_out, cotan):
    routed = picks.shape[0]
    width = tokens.shape[1]
    n_tok = tokens.shape[0]
    hid = w_in.shape[1]
    half = hid // 2
    ctx = lax.axis_index("ctx")
    px, py = ctx // SIDE, ctx % SIDE
    quarter = width // SIDE
    sixteenth = quarter // SIDE

    live = (jnp.arange(routed, dtype=jnp.int32) < counts[0])[:, None]
    place = picks[:, None] == jnp.arange(n_tok, dtype=jnp.int32)[None, :]
    rows = dot((place & live).astype(BF16), tokens, ((1,), (0,))).astype(BF16)
    dffn = (score[:, None] * cotan.astype(F32) * live.astype(F32)).astype(BF16)
    own = jnp.stack([rows, dffn])

    below = move_z(own, 1)
    above = move_z(own, -1)
    own_other = swap_core(own)
    far = jnp.concatenate(
        [move_z(below[:, : routed // 2], 1), move_z(above[:, routed // 2 :], -1)], axis=1
    )
    near_other = swap_core(jnp.stack([below, above]))
    far_other = swap_core(far)

    def work(mine, other):
        r = jnp.concatenate([mine[0], other[0]], axis=0)
        d = jnp.concatenate([mine[1], other[1]], axis=0)
        pre = dot(r, w_in, ((1,), (0,)))
        value, slope = gelu_parts(pre)
        hidden = value.astype(BF16)
        dpre = (dot(d, w_out, ((1,), (1,))) * slope).astype(BF16)
        ffn = dot(hidden, w_out, ((1,), (0,)))
        dx = dot(dpre, w_in, ((1,), (1,)))
        return r, d, hidden, dpre, jnp.stack([ffn[:routed], dx[:routed]]), jnp.stack([ffn[routed:], dx[routed:]])

    parts = [work(own, own_other), work(below, near_other[0]), work(above, near_other[1]), work(far, far_other)]
    all_rows, all_dffn, hidden, dpre = (jnp.concatenate([p[i] for p in parts], axis=0) for i in range(4))

    def chip_sum(p):
        return p[4] + swap_core(p[5].astype(BF16)).astype(F32)

    sums = [chip_sum(p) for p in parts]
    back = (
        sums[0]
        + move_z(sums[1].astype(BF16), -1).astype(F32)
        + move_z(sums[2].astype(BF16), 1).astype(F32)
        + move_z(sums[3].astype(BF16), 2).astype(F32)
    ).astype(BF16)

    def halves(a):
        return a[:, :half], a[:, half:]

    dpre_h, hidden_h = halves(dpre), halves(hidden)

    def in_term(k, p):
        cols = lax.dynamic_slice_in_dim(all_rows, ((px + k) % SIDE) * quarter, quarter, axis=1)
        return dot(cols, dpre_h[p], ((0,), (0,)))

    dffn_tiles = all_dffn.reshape(all_dffn.shape[0], SIDE, SIDE, sixteenth)

    def out_term(k, p):
        cols = lax.dynamic_index_in_dim(dffn_tiles, (py + k) % SIDE, axis=2, keepdims=False)
        return dot(hidden_h[p], cols.reshape(all_dffn.shape[0], quarter), ((0,), (0,)))

    a0, a1 = ring_scatter(in_term, move_x)
    b0, b1 = ring_scatter(out_term, move_y)
    a = jnp.concatenate([a0, a1], axis=1)
    b = jnp.concatenate([b0, b1], axis=0)
    grad_in = direct_scatter(
        lambda k: lax.dynamic_slice_in_dim(a, ((py + k) % SIDE) * sixteenth, sixteenth, axis=0), move_y
    )
    grad_out = direct_scatter(
        lambda k: lax.dynamic_slice_in_dim(b, ((px + k) % SIDE) * sixteenth, sixteenth, axis=1), move_x
    )

    ffn = back[0].astype(F32)
    heavy = (score[:, None] * ffn).astype(BF16)
    grad_score = jnp.sum(cotan.astype(F32) * ffn, axis=1)
    grad_x = dot(place.astype(BF16), back[1], ((0,), (0,))).astype(BF16)
    return (heavy, grad_x, grad_score, grad_in, grad_out)


def solution(mesh):
    placed = (
        P(("ctx", "head"), None),
        P(("ctx", "head")),
        P(("ctx", "head")),
        P(("ctx", "head")),
        P(None, "head"),
        P("head", None),
        P(("ctx", "head"), None),
    )
    return jax.shard_map(
        on_device,
        mesh=mesh,
        in_specs=placed,
        out_specs=(
            P(("ctx", "head"), None),
            P(("ctx", "head"), None),
            P(("ctx", "head")),
            P("ctx", "head"),
            P("head", "ctx"),
        ),
        check_vma=False,
    )
```

```python
import functools

import jax
import jax.numpy as jnp
from jax import lax
from jax.experimental import pallas as pl
from jax.experimental.pallas import tpu as pltpu
from jax.sharding import PartitionSpec as P

F32 = jnp.float32
BF16 = jnp.bfloat16
SIDE = 4
MIB = 1024 * 1024
LITTLE = pl.CostEstimate(flops=1, bytes_accessed=1, transcendentals=0)


def gelu_parts(u):
    c = 0.7978845608
    t = jnp.tanh(c * (u + 0.044715 * u * u * u))
    value = 0.5 * u * (1.0 + t)
    slope = 0.5 * (1.0 + t) + 0.5 * u * (1.0 - t * t) * c * (1.0 + 3.0 * 0.044715 * u * u)
    return (value, slope)


def move_x(v, by):
    perm = [(x * SIDE + y, ((x + by) % SIDE) * SIDE + y) for x in range(SIDE) for y in range(SIDE)]
    return lax.ppermute(v, "ctx", perm)


def move_y(v, by):
    perm = [(x * SIDE + y, x * SIDE + (y + by) % SIDE) for x in range(SIDE) for y in range(SIDE)]
    return lax.ppermute(v, "ctx", perm)


def move_lane(v, by):
    perm = [(z * 2 + c, ((z + (by if c == 0 else -by)) % SIDE) * 2 + c) for z in range(SIDE) for c in range(2)]
    return lax.ppermute(v, "head", perm)


def swap_core(v):
    return lax.ppermute(v, "head", [(i, i ^ 1) for i in range(2 * SIDE)])


def dot(a, b, dims):
    return lax.dot_general(a, b, ((dims[0], dims[1]), ((), ())), preferred_element_type=F32)


def params(mib):
    return pltpu.CompilerParams(vmem_limit_bytes=mib * MIB)


def whole(a):
    return pl.BlockSpec(a.shape, lambda *_: (0,) * a.ndim)


def take_rows(tokens, picks, counts, score, cotan):
    routed = picks.shape[0]
    n_tok, width = tokens.shape

    def body(counts_ref, tokens_ref, picks_ref, score_ref, cotan_ref, out_ref, me_ref):
        me_ref[0] = lax.axis_index("ctx").astype(jnp.int32)
        me_ref[1] = lax.axis_index("head").astype(jnp.int32)
        places = lax.broadcasted_iota(jnp.int32, (n_tok, routed), 0)
        slots = lax.broadcasted_iota(jnp.int32, (n_tok, routed), 1)
        hit = (places == picks_ref[...]) & (slots < counts_ref[0])
        one_hot = jnp.where(hit, 1.0, 0.0).astype(BF16)
        out_ref[0] = dot(one_hot, tokens_ref[...], ((0,), (0,))).astype(BF16)
        across = lax.broadcasted_iota(jnp.int32, (routed, routed), 0)
        along = lax.broadcasted_iota(jnp.int32, (routed, routed), 1)
        kept = (across == along) & (along < counts_ref[0])
        factor = jnp.sum(jnp.where(kept, score_ref[...], 0.0), axis=1, keepdims=True)
        out_ref[1] = (factor * cotan_ref[...].astype(F32)).astype(BF16)

    return pl.pallas_call(
        body,
        grid_spec=pltpu.PrefetchScalarGridSpec(
            num_scalar_prefetch=1,
            grid=(1,),
            in_specs=[
                whole(tokens),
                pl.BlockSpec((1, routed), lambda i, c: (0, 0)),
                pl.BlockSpec((1, routed), lambda i, c: (0, 0)),
                whole(cotan),
            ],
            out_specs=[
                pl.BlockSpec((2, routed, width), lambda i, c: (0, 0, 0)),
                pl.BlockSpec(memory_space=pltpu.SMEM),
            ],
        ),
        out_shape=[jax.ShapeDtypeStruct((2, routed, width), BF16), jax.ShapeDtypeStruct((2,), jnp.int32)],
        compiler_params=params(60),
        cost_estimate=LITTLE,
        name="take_rows",
    )(counts, tokens, picks[None, :], score[None, :], cotan)


def hidden_units(packs, w_in, w_out):
    n = len(packs)
    _, piece, width = packs[0].shape
    count = n * piece
    hid = w_in.shape[1]
    tile = hid // SIDE
    quarter = width // SIDE
    strip = quarter // SIDE

    def body(*refs):
        r = jnp.concatenate([ref[0] for ref in refs[:n]], axis=0)
        d = jnp.concatenate([ref[1] for ref in refs[:n]], axis=0)
        win_ref, wout_ref, hidden_ref, dpre_ref, turned_ref = refs[n:]
        pre = dot(r, win_ref[...], ((1,), (0,)))
        dhid = dot(d, wout_ref[...], ((1,), (1,)))
        value, slope = gelu_parts(pre)
        hidden_ref[...] = value.astype(BF16)
        dpre_ref[...] = (dhid * slope).astype(BF16)
        y = pl.program_id(0)
        for x in range(SIDE):
            at = pl.multiple_of(x * quarter + y * strip, strip)
            for k in range(n):
                turned_ref[pl.ds(k * piece, piece), pl.ds(x * strip, strip)] = refs[k][1, :, pl.ds(at, strip)]

    return pl.pallas_call(
        body,
        grid=(SIDE,),
        in_specs=[whole(a) for a in packs]
        + [
            pl.BlockSpec((width, tile), lambda j: (0, j)),
            pl.BlockSpec((tile, width), lambda j: (j, 0)),
        ],
        out_specs=[
            pl.BlockSpec((count, tile), lambda j: (0, j)),
            pl.BlockSpec((count, tile), lambda j: (0, j)),
            pl.BlockSpec((count, quarter), lambda j: (0, j)),
        ],
        out_shape=[
            jax.ShapeDtypeStruct((count, hid), BF16),
            jax.ShapeDtypeStruct((count, hid), BF16),
            jax.ShapeDtypeStruct((count, width), BF16),
        ],
        compiler_params=params(4 + count // 64),
        cost_estimate=LITTLE,
        name="hidden_units",
    )(*packs, held(w_in), held(w_out))


def hold(w_in, w_out):
    def body(win_ref, wout_ref, win_out, wout_out, sems):
        copies = [
            pltpu.make_async_copy(win_ref, win_out, sems.at[0]),
            pltpu.make_async_copy(wout_ref, wout_out, sems.at[1]),
        ]
        for copy in copies:
            copy.start()
        for copy in copies:
            copy.wait()

    return pl.pallas_call(
        body,
        in_specs=[pl.BlockSpec(memory_space=pl.ANY)] * 2,
        out_specs=[pl.BlockSpec(memory_space=pltpu.VMEM)] * 2,
        out_shape=[pltpu.VMEM(w.shape, w.dtype) for w in (w_in, w_out)],
        scratch_shapes=[pltpu.SemaphoreType.DMA((2,))],
        compiler_params=params(4),
        cost_estimate=LITTLE,
        name="hold_weights",
    )(pltpu.with_memory_space_constraint(w_in, pltpu.HBM), pltpu.with_memory_space_constraint(w_out, pltpu.HBM))


def held(w):
    return pltpu.with_memory_space_constraint(w, pltpu.VMEM)


def in_hbm(arrays):
    return [pltpu.with_memory_space_constraint(a, pltpu.HBM) for a in arrays]


def owners(head):
    chip, core = head // 2, lax.rem(head, 2)
    back = 1 + 2 * core
    here, behind = chip, lax.rem(chip + SIDE - back, SIDE)
    ahead, far = lax.rem(chip + back, SIDE), lax.rem(chip + 2, SIDE)
    rest = 1 - core
    return [
        here * 2 + core, here * 2 + rest,
        behind * 2 + core, ahead * 2 + rest,
        behind * 2 + rest, ahead * 2 + core,
        far * 2 + core, far * 2 + rest,
    ]


def row_terms(hidden, dpre, w_in, w_out, piece):
    count, hid = hidden.shape
    width = w_in.shape[0]
    n = count // piece
    tile = width // SIDE

    def body(hidden_ref, dpre_ref, win_ref, wout_ref, out_ref):
        ffn = dot(hidden_ref[...], wout_ref[...], ((1,), (0,))).astype(BF16)
        dx = dot(dpre_ref[...], win_ref[...], ((1,), (1,))).astype(BF16)
        for s, v in enumerate((ffn, dx)):
            for k in range(n):
                out_ref[k, s] = v[k * piece : (k + 1) * piece]

    return pl.pallas_call(
        body,
        grid=(SIDE,),
        in_specs=[
            whole(hidden),
            whole(dpre),
            pl.BlockSpec((tile, hid), lambda j: (j, 0)),
            pl.BlockSpec((hid, tile), lambda j: (0, j)),
        ],
        out_specs=pl.BlockSpec((n, 2, piece, tile), lambda j: (0, 0, 0, j)),
        out_shape=jax.ShapeDtypeStruct((n, 2, piece, width), BF16),
        compiler_params=params(8),
        cost_estimate=LITTLE,
        name="row_terms",
    )(hidden, dpre, held(w_in), held(w_out))


def all_terms(me, earlier, hidden, dpre, w_in, w_out, piece):
    count, hid = hidden.shape
    width = w_in.shape[0]
    n = count // piece
    tile = width // SIDE
    total = n + sum(a.shape[0] for a in earlier)

    def body(me_ref, *refs):
        hidden_ref, dpre_ref, win_ref, wout_ref, out_ref = refs[len(earlier) :]
        to = owners(me_ref[1])
        at = 0
        for ref in refs[: len(earlier)]:
            for k in range(ref.shape[0]):
                out_ref[to[at]] = ref[k]
                at += 1
        ffn = dot(hidden_ref[...], wout_ref[...], ((1,), (0,))).astype(BF16)
        dx = dot(dpre_ref[...], win_ref[...], ((1,), (1,))).astype(BF16)
        for k in range(n):
            for s, v in enumerate((ffn, dx)):
                out_ref[to[at + k], s] = v[k * piece : (k + 1) * piece]

    def terms(a):
        return pl.BlockSpec((a.shape[0], 2, piece, tile), lambda j, h: (0, 0, 0, j))

    return pl.pallas_call(
        body,
        grid_spec=pltpu.PrefetchScalarGridSpec(
            num_scalar_prefetch=1,
            grid=(SIDE,),
            in_specs=[terms(a) for a in earlier]
            + [
                whole(hidden),
                whole(dpre),
                pl.BlockSpec((tile, hid), lambda j, h: (j, 0)),
                pl.BlockSpec((hid, tile), lambda j, h: (0, j)),
            ],
            out_specs=pl.BlockSpec((total, 2, piece, tile), lambda j, h: (0, 0, 0, j)),
        ),
        out_shape=pltpu.HBM((total, 2, piece, width), BF16),
        compiler_params=params(14),
        cost_estimate=LITTLE,
        name="all_terms",
    )(me, *earlier, hidden, dpre, held(w_in), held(w_out))


def first_step(i):
    place = jnp.where(i < 2, 2, jnp.where(i == 2, 1, 3))
    half = jnp.where((i == 1) | (i == 2), 1, 0)
    return place, half


def later_step(i):
    place = jnp.where(i >= 2, 0, jnp.where(i == 0, 1, 3))
    half = jnp.where((i == 1) | (i == 3), 1, 0)
    return place, half


def in_blocks(me, packs, dpre, order, split):
    n = len(packs)
    _, piece, width = packs[0].shape
    hid = dpre[0].shape[1]
    size = width // (2 * SIDE)

    def body(me_ref, *refs):
        i = pl.program_id(0)
        r = jnp.concatenate([ref[0] for ref in refs[:n]], axis=0)
        d = jnp.concatenate([ref[...] for ref in refs[n : n + len(dpre)]], axis=0)
        term = dot(r, d, ((0,), (0,))).astype(BF16)
        outs = refs[n + len(dpre) :]
        if split:
            for s in range(2):

                @pl.when(lax.rem(i, 2) == s)
                def _():
                    outs[s][0] = term

        else:
            outs[0][0] = term

    def columns(i, me_ref):
        place, half = order(i)
        return (0, 0, 2 * lax.rem(me_ref[0] // SIDE + place, SIDE) + half)

    return blocks_call(body, me, [pl.BlockSpec((1, piece, size), columns)] * n + [whole(a) for a in dpre],
                       in_hbm(packs + dpre), (size, hid), split, n * piece)


def out_blocks(me, hidden, turned, order, split):
    count = sum(a.shape[0] for a in hidden)
    hid = hidden[0].shape[1]
    quarter = turned[0].shape[1] // SIDE

    def body(me_ref, *refs):
        i = pl.program_id(0)
        n = len(hidden)
        h = jnp.concatenate([ref[...] for ref in refs[:n]], axis=0)
        d = jnp.concatenate([ref[...] for ref in refs[n : 2 * n]], axis=0)
        term = dot(h, d, ((0,), (0,))).astype(BF16)
        outs = refs[2 * n :]
        if split:
            for s in range(2):

                @pl.when(lax.rem(i, 2) == s)
                def _():
                    outs[s][0] = term

        else:
            outs[0][0] = term

    def units(i, me_ref):
        return (0, order(i)[1])

    def columns(i, me_ref):
        return (0, lax.rem(lax.rem(me_ref[0], SIDE) + order(i)[0], SIDE))

    specs = [pl.BlockSpec((a.shape[0], hid // 2), units) for a in hidden]
    specs += [pl.BlockSpec((a.shape[0], quarter), columns) for a in turned]
    return blocks_call(body, me, specs, in_hbm(hidden + turned), (hid // 2, quarter), split, count)


def blocks_call(body, me, specs, args, block, split, count):
    if split:
        shapes = [jax.ShapeDtypeStruct((2,) + block, BF16)] * 2
        outs = [pl.BlockSpec((1,) + block, lambda i, me_ref: (i // 2, 0, 0))] * 2
    else:
        shapes = [jax.ShapeDtypeStruct((4,) + block, BF16)]
        outs = [pl.BlockSpec((1,) + block, lambda i, me_ref: (i, 0, 0))]
    return pl.pallas_call(
        body,
        grid_spec=pltpu.PrefetchScalarGridSpec(
            num_scalar_prefetch=1, grid=(4,), in_specs=specs, out_specs=outs
        ),
        out_shape=shapes,
        compiler_params=params(8),
        cost_estimate=LITTLE,
        name="weight_blocks",
    )(me, *args)


def ring_total(me, later, below0, above0, below1, above1, rowwise):
    block = later.shape[1:]
    if rowwise:
        cut = (2 * block[0] // SIDE, block[1])
    else:
        cut = (2 * block[0], block[1] // SIDE)

    def body(me_ref, later_ref, b0, a0, b1, a1, keep_ref, next_ref, prev_ref, far_ref, sum_ref):
        half = block[0]
        sum_ref[pl.ds(0, half), :] = later_ref[0].astype(F32) + b0[...].astype(F32) + a0[0].astype(F32)
        sum_ref[pl.ds(half, half), :] = later_ref[1].astype(F32) + b1[0].astype(F32) + a1[...].astype(F32)
        if rowwise:
            at = lax.rem(me_ref[0], SIDE)
        else:
            at = me_ref[0] // SIDE
        for k, ref in ((0, keep_ref), (1, next_ref), (3, prev_ref), (2, far_ref)):
            to = lax.rem(at + k, SIDE)
            if rowwise:
                v = sum_ref[pl.ds(pl.multiple_of(to * cut[0], cut[0]), cut[0]), :]
            else:
                v = sum_ref[:, pl.ds(pl.multiple_of(to * cut[1], cut[1]), cut[1])]
            ref[...] = v.astype(ref.dtype)

    second = pl.BlockSpec((2,) + block, lambda i, me_ref: (1, 0, 0))
    one = pl.BlockSpec(block, lambda i, me_ref: (0, 0))
    tail = pl.BlockSpec((1,) + block, lambda i, me_ref: (1, 0, 0))
    out = pl.BlockSpec(cut, lambda i, me_ref: (0, 0))
    return pl.pallas_call(
        body,
        grid_spec=pltpu.PrefetchScalarGridSpec(
            num_scalar_prefetch=1,
            grid=(1,),
            in_specs=[second, one, tail, tail, one],
            out_specs=[out] * 4,
            scratch_shapes=[pltpu.VMEM((2 * block[0], block[1]), F32)],
        ),
        out_shape=[jax.ShapeDtypeStruct(cut, F32)] + [jax.ShapeDtypeStruct(cut, BF16)] * 3,
        compiler_params=params(8),
        cost_estimate=LITTLE,
        name="ring_total",
    )(me, later, below0, above0, below1, above1)


def after(values, *deps):
    return lax.optimization_barrier((values, deps))[0]


def on_device(tokens, picks, counts, score, w_in, w_out, cotan):
    routed = picks.shape[0]
    n_tok = tokens.shape[0]

    own_mine, me = take_rows(tokens, picks, counts, score, cotan)
    w_in, w_out = hold(*after((w_in, w_out), own_mine))
    near_mine = move_lane(own_mine, 1)
    own_other = swap_core(own_mine)
    own_packs = [own_mine, own_other]
    own = hidden_units(own_packs, w_in, w_out)

    near_other = move_lane(own_other, 1)
    near_mine = after(near_mine, own)
    far_mine = move_lane(near_mine, 1)
    near_packs = [near_mine, swap_core(near_mine)]
    near = hidden_units(near_packs, w_in, w_out)
    own_terms = row_terms(own[0], own[1], w_in, w_out, routed)
    near_terms = row_terms(near[0], near[1], w_in, w_out, routed)

    near_other, far_mine = after((near_other, far_mine), near, own_terms, near_terms)
    last_packs = [near_other, swap_core(near_other), far_mine, swap_core(far_mine)]
    last = hidden_units(last_packs, w_in, w_out)
    terms = all_terms(me, [own_terms, near_terms], last[0], last[1], w_in, w_out, routed)
    width = tokens.shape[1]
    sums = lax.psum_scatter(terms.reshape(-1, width), "head", scatter_dimension=0, tiled=True)

    all_packs = own_packs + near_packs + last_packs
    hidden, dpre, turned = ([u[i] for u in (own, near, last)] for i in range(3))
    all_packs, dpre = after((all_packs, dpre), terms)
    in_up, in_down = in_blocks(me, all_packs, dpre, first_step, True)
    in_below, in_above = move_x(in_up, 1), move_x(in_down, -1)
    hidden, turned = after((hidden, turned), in_up, in_down)
    out_up, out_down = out_blocks(me, hidden, turned, first_step, True)
    out_below, out_above = move_y(out_up, 1), move_y(out_down, -1)

    all_packs, dpre = after((all_packs, dpre), out_up, out_down)
    in_later = in_blocks(me, all_packs, dpre, later_step, False)[0]
    hidden, turned = after((hidden, turned), in_later)
    out_later = out_blocks(me, hidden, turned, later_step, False)[0]

    def second_hop(later, from_below, from_above, move):
        up = (later[0].astype(F32) + from_below[0].astype(F32)).astype(BF16)
        down = (later[1].astype(F32) + from_above[0].astype(F32)).astype(BF16)
        return move(up, 1), move(down, -1), up, down

    in_below, in_above = after((in_below, in_above), out_later)
    in_hops = second_hop(in_later, in_below, in_above, move_x)
    out_below, out_above = after((out_below, out_above), in_hops[2:])
    out_hops = second_hop(out_later, out_below, out_above, move_y)

    def second_stage(total, move):
        keep, following, previous, far = total
        return keep, move(far, 2), move(following, 1), move(previous, -1)

    def add_up(parts):
        return parts[0] + parts[1].astype(F32) + parts[2].astype(F32) + parts[3].astype(F32)

    in_total = ring_total(me, in_later, in_hops[0], in_above, in_below, in_hops[1], True)
    in_parts = second_stage(in_total, move_y)
    out_hops = after(out_hops[:2], in_total)
    out_total = ring_total(me, out_later, out_hops[0], out_above, out_below, out_hops[1], False)
    out_parts = second_stage(out_total, move_x)

    sums = after(sums, out_total)
    ffn = sums[:routed].astype(F32)
    heavy = (score[:, None] * ffn).astype(BF16)
    grad_score = jnp.sum(cotan.astype(F32) * ffn, axis=1)
    place = picks[:, None] == jnp.arange(n_tok, dtype=jnp.int32)[None, :]
    grad_x = dot(place.astype(BF16), sums[routed:], ((0,), (0,))).astype(BF16)
    in_parts, out_parts = after((in_parts, out_parts), heavy, grad_x)
    grad_in = add_up(in_parts)
    grad_out = add_up(out_parts)
    return (heavy, grad_x, grad_score, grad_in, grad_out)


def solution(mesh):
    placed = (
        P(("ctx", "head"), None),
        P(("ctx", "head")),
        P(("ctx", "head")),
        P(("ctx", "head")),
        P(None, "head"),
        P("head", None),
        P(("ctx", "head"), None),
    )
    return jax.shard_map(
        on_device,
        mesh=mesh,
        in_specs=placed,
        out_specs=(
            P(("ctx", "head"), None),
            P(("ctx", "head"), None),
            P(("ctx", "head")),
            P("ctx", "head"),
            P("head", "ctx"),
        ),
        check_vma=False,
    )
```

```python
import functools

import jax
import jax.numpy as jnp
from jax import lax
from jax.experimental import pallas as pl
from jax.experimental.pallas import tpu as pltpu
from jax.sharding import PartitionSpec as P

F32 = jnp.float32
BF16 = jnp.bfloat16
SIDE = 4
MIB = 1024 * 1024
LITTLE = pl.CostEstimate(flops=1, bytes_accessed=1, transcendentals=0)


def gelu_parts(u):
    c = 0.7978845608
    t = jnp.tanh(c * (u + 0.044715 * u * u * u))
    value = 0.5 * u * (1.0 + t)
    slope = 0.5 * (1.0 + t) + 0.5 * u * (1.0 - t * t) * c * (1.0 + 3.0 * 0.044715 * u * u)
    return (value, slope)


def move_x(v, by):
    perm = [(x * SIDE + y, ((x + by) % SIDE) * SIDE + y) for x in range(SIDE) for y in range(SIDE)]
    return lax.ppermute(v, "ctx", perm)


def move_y(v, by):
    perm = [(x * SIDE + y, x * SIDE + (y + by) % SIDE) for x in range(SIDE) for y in range(SIDE)]
    return lax.ppermute(v, "ctx", perm)


def move_lane(v, by):
    perm = [(z * 2 + c, ((z + (by if c == 0 else -by)) % SIDE) * 2 + c) for z in range(SIDE) for c in range(2)]
    return lax.ppermute(v, "head", perm)


def swap_core(v):
    return lax.ppermute(v, "head", [(i, i ^ 1) for i in range(2 * SIDE)])


def dot(a, b, dims):
    return lax.dot_general(a, b, ((dims[0], dims[1]), ((), ())), preferred_element_type=F32)


def params(mib):
    return pltpu.CompilerParams(vmem_limit_bytes=mib * MIB)


def whole(a):
    return pl.BlockSpec(a.shape, lambda *_: (0,) * a.ndim)


def take_rows(tokens, picks, counts, score, cotan):
    routed = picks.shape[0]
    n_tok, width = tokens.shape

    def body(counts_ref, tokens_ref, picks_ref, score_ref, cotan_ref, out_ref, me_ref):
        me_ref[0] = lax.axis_index("ctx").astype(jnp.int32)
        me_ref[1] = lax.axis_index("head").astype(jnp.int32)
        places = lax.broadcasted_iota(jnp.int32, (n_tok, routed), 0)
        slots = lax.broadcasted_iota(jnp.int32, (n_tok, routed), 1)
        hit = (places == picks_ref[...]) & (slots < counts_ref[0])
        one_hot = jnp.where(hit, 1.0, 0.0).astype(BF16)
        out_ref[0] = dot(one_hot, tokens_ref[...], ((0,), (0,))).astype(BF16)
        across = lax.broadcasted_iota(jnp.int32, (routed, routed), 0)
        along = lax.broadcasted_iota(jnp.int32, (routed, routed), 1)
        kept = (across == along) & (along < counts_ref[0])
        factor = jnp.sum(jnp.where(kept, score_ref[...], 0.0), axis=1, keepdims=True)
        out_ref[1] = (factor * cotan_ref[...].astype(F32)).astype(BF16)

    return pl.pallas_call(
        body,
        grid_spec=pltpu.PrefetchScalarGridSpec(
            num_scalar_prefetch=1,
            grid=(1,),
            in_specs=[
                whole(tokens),
                pl.BlockSpec((1, routed), lambda i, c: (0, 0)),
                pl.BlockSpec((1, routed), lambda i, c: (0, 0)),
                whole(cotan),
            ],
            out_specs=[
                pl.BlockSpec((2, routed, width), lambda i, c: (0, 0, 0)),
                pl.BlockSpec(memory_space=pltpu.SMEM),
            ],
        ),
        out_shape=[jax.ShapeDtypeStruct((2, routed, width), BF16), jax.ShapeDtypeStruct((2,), jnp.int32)],
        compiler_params=params(60),
        cost_estimate=LITTLE,
        name="take_rows",
    )(counts, tokens, picks[None, :], score[None, :], cotan)


def hidden_units(packs, w_in, w_out):
    n = len(packs)
    _, piece, width = packs[0].shape
    count = n * piece
    hid = w_in.shape[1]
    tile = hid // SIDE
    quarter = width // SIDE
    strip = quarter // SIDE

    def body(*refs):
        r = jnp.concatenate([ref[0] for ref in refs[:n]], axis=0)
        d = jnp.concatenate([ref[1] for ref in refs[:n]], axis=0)
        win_ref, wout_ref, hidden_ref, dpre_ref, turned_ref = refs[n:]
        pre = dot(r, win_ref[...], ((1,), (0,)))
        dhid = dot(d, wout_ref[...], ((1,), (1,)))
        value, slope = gelu_parts(pre)
        hidden_ref[...] = value.astype(BF16)
        dpre_ref[...] = (dhid * slope).astype(BF16)
        y = pl.program_id(0)
        for x in range(SIDE):
            at = pl.multiple_of(x * quarter + y * strip, strip)
            for k in range(n):
                turned_ref[pl.ds(k * piece, piece), pl.ds(x * strip, strip)] = refs[k][1, :, pl.ds(at, strip)]

    return pl.pallas_call(
        body,
        grid=(SIDE,),
        in_specs=[whole(a) for a in packs]
        + [
            pl.BlockSpec((width, tile), lambda j: (0, j)),
            pl.BlockSpec((tile, width), lambda j: (j, 0)),
        ],
        out_specs=[
            pl.BlockSpec((count, tile), lambda j: (0, j)),
            pl.BlockSpec((count, tile), lambda j: (0, j)),
            pl.BlockSpec((count, quarter), lambda j: (0, j)),
        ],
        out_shape=[
            jax.ShapeDtypeStruct((count, hid), BF16),
            jax.ShapeDtypeStruct((count, hid), BF16),
            jax.ShapeDtypeStruct((count, width), BF16),
        ],
        compiler_params=params(4 + count // 64),
        cost_estimate=LITTLE,
        name="hidden_units",
    )(*packs, held(w_in), held(w_out))


def hold(w_in, w_out):
    def body(win_ref, wout_ref, win_out, wout_out, sems):
        copies = [
            pltpu.make_async_copy(win_ref, win_out, sems.at[0]),
            pltpu.make_async_copy(wout_ref, wout_out, sems.at[1]),
        ]
        for copy in copies:
            copy.start()
        for copy in copies:
            copy.wait()

    return pl.pallas_call(
        body,
        in_specs=[pl.BlockSpec(memory_space=pl.ANY)] * 2,
        out_specs=[pl.BlockSpec(memory_space=pltpu.VMEM)] * 2,
        out_shape=[pltpu.VMEM(w.shape, w.dtype) for w in (w_in, w_out)],
        scratch_shapes=[pltpu.SemaphoreType.DMA((2,))],
        compiler_params=params(4),
        cost_estimate=LITTLE,
        name="hold_weights",
    )(pltpu.with_memory_space_constraint(w_in, pltpu.HBM), pltpu.with_memory_space_constraint(w_out, pltpu.HBM))


def held(w):
    return pltpu.with_memory_space_constraint(w, pltpu.VMEM)


def row_terms(hidden, dpre, w_in, w_out, piece, groups, held_terms=()):
    count, hid = hidden.shape
    width = w_in.shape[0]
    n = count // (2 * piece)
    tile = width // SIDE

    def body(hidden_ref, dpre_ref, win_ref, wout_ref, *refs):
        outs = refs[len(held_terms) :]
        ffn = dot(hidden_ref[...], wout_ref[...], ((1,), (0,))).astype(BF16)
        dx = dot(dpre_ref[...], win_ref[...], ((1,), (1,))).astype(BF16)
        for h in range(2):
            for k in range(n):
                for s, v in enumerate((ffn, dx)):
                    outs[h][k, s] = v[(h * n + k) * piece : (h * n + k + 1) * piece]

    first = groups - 1 if held_terms else 0
    return pl.pallas_call(
        body,
        grid=(SIDE,),
        in_specs=[
            whole(hidden),
            whole(dpre),
            pl.BlockSpec((tile, hid), lambda j: (j, 0)),
            pl.BlockSpec((hid, tile), lambda j: (0, j)),
        ]
        + [pl.BlockSpec(memory_space=pl.ANY)] * len(held_terms),
        out_specs=[pl.BlockSpec((n, 2, piece, tile), lambda j: (first, 0, 0, j))] * 2,
        out_shape=[jax.ShapeDtypeStruct((groups, 2, piece, width), BF16)] * 2,
        input_output_aliases={4 + i: i for i in range(len(held_terms))},
        compiler_params=params(6 + count // 64),
        cost_estimate=LITTLE,
        name="row_terms",
    )(hidden, dpre, held(w_in), held(w_out), *held_terms)


def first_step(i):
    place = jnp.where(i < 2, 2, jnp.where(i == 2, 1, 3))
    half = jnp.where((i == 1) | (i == 2), 1, 0)
    return place, half


def later_step(i):
    place = jnp.where(i >= 2, 0, jnp.where(i == 0, 1, 3))
    half = jnp.where((i == 1) | (i == 3), 1, 0)
    return place, half


def in_blocks(me, packs, dpre, order, split):
    n = len(packs)
    _, piece, width = packs[0].shape
    hid = dpre[0].shape[1]
    size = width // (2 * SIDE)

    def body(me_ref, *refs):
        i = pl.program_id(0)
        r = jnp.concatenate([ref[0] for ref in refs[:n]], axis=0)
        d = jnp.concatenate([ref[...] for ref in refs[n : n + len(dpre)]], axis=0)
        term = dot(r, d, ((0,), (0,))).astype(BF16)
        outs = refs[n + len(dpre) :]
        if split:
            for s in range(2):

                @pl.when(lax.rem(i, 2) == s)
                def _():
                    outs[s][0] = term

        else:
            outs[0][0] = term

    def columns(i, me_ref):
        place, half = order(i)
        return (0, 0, 2 * lax.rem(me_ref[0] // SIDE + place, SIDE) + half)

    return blocks_call(body, me, [pl.BlockSpec((1, piece, size), columns)] * n + [whole(a) for a in dpre],
                       packs + dpre, (size, hid), split, n * piece)


def out_blocks(me, hidden, turned, order, split):
    count = sum(a.shape[0] for a in hidden)
    hid = hidden[0].shape[1]
    quarter = turned[0].shape[1] // SIDE

    def body(me_ref, *refs):
        i = pl.program_id(0)
        n = len(hidden)
        h = jnp.concatenate([ref[...] for ref in refs[:n]], axis=0)
        d = jnp.concatenate([ref[...] for ref in refs[n : 2 * n]], axis=0)
        term = dot(h, d, ((0,), (0,))).astype(BF16)
        outs = refs[2 * n :]
        if split:
            for s in range(2):

                @pl.when(lax.rem(i, 2) == s)
                def _():
                    outs[s][0] = term

        else:
            outs[0][0] = term

    def units(i, me_ref):
        return (0, order(i)[1])

    def columns(i, me_ref):
        return (0, lax.rem(lax.rem(me_ref[0], SIDE) + order(i)[0], SIDE))

    specs = [pl.BlockSpec((a.shape[0], hid // 2), units) for a in hidden]
    specs += [pl.BlockSpec((a.shape[0], quarter), columns) for a in turned]
    return blocks_call(body, me, specs, hidden + turned, (hid // 2, quarter), split, count)


def blocks_call(body, me, specs, args, block, split, count):
    if split:
        shapes = [jax.ShapeDtypeStruct((2,) + block, BF16)] * 2
        outs = [pl.BlockSpec((1,) + block, lambda i, me_ref: (i // 2, 0, 0))] * 2
    else:
        shapes = [jax.ShapeDtypeStruct((4,) + block, BF16)]
        outs = [pl.BlockSpec((1,) + block, lambda i, me_ref: (i, 0, 0))]
    return pl.pallas_call(
        body,
        grid_spec=pltpu.PrefetchScalarGridSpec(
            num_scalar_prefetch=1, grid=(4,), in_specs=specs, out_specs=outs
        ),
        out_shape=shapes,
        compiler_params=params(8),
        cost_estimate=LITTLE,
        name="weight_blocks",
    )(me, *args)


def ring_total(me, later, below0, above0, below1, above1, rowwise):
    block = later.shape[1:]
    if rowwise:
        cut = (2 * block[0] // SIDE, block[1])
    else:
        cut = (2 * block[0], block[1] // SIDE)

    def body(me_ref, later_ref, b0, a0, b1, a1, keep_ref, next_ref, prev_ref, far_ref, sum_ref):
        half = block[0]
        sum_ref[pl.ds(0, half), :] = later_ref[0].astype(F32) + b0[...].astype(F32) + a0[0].astype(F32)
        sum_ref[pl.ds(half, half), :] = later_ref[1].astype(F32) + b1[0].astype(F32) + a1[...].astype(F32)
        if rowwise:
            at = lax.rem(me_ref[0], SIDE)
        else:
            at = me_ref[0] // SIDE
        for k, ref in ((0, keep_ref), (1, next_ref), (3, prev_ref), (2, far_ref)):
            to = lax.rem(at + k, SIDE)
            if rowwise:
                v = sum_ref[pl.ds(pl.multiple_of(to * cut[0], cut[0]), cut[0]), :]
            else:
                v = sum_ref[:, pl.ds(pl.multiple_of(to * cut[1], cut[1]), cut[1])]
            ref[...] = v.astype(ref.dtype)

    second = pl.BlockSpec((2,) + block, lambda i, me_ref: (1, 0, 0))
    one = pl.BlockSpec(block, lambda i, me_ref: (0, 0))
    tail = pl.BlockSpec((1,) + block, lambda i, me_ref: (1, 0, 0))
    out = pl.BlockSpec(cut, lambda i, me_ref: (0, 0))
    return pl.pallas_call(
        body,
        grid_spec=pltpu.PrefetchScalarGridSpec(
            num_scalar_prefetch=1,
            grid=(1,),
            in_specs=[second, one, tail, tail, one],
            out_specs=[out] * 4,
            scratch_shapes=[pltpu.VMEM((2 * block[0], block[1]), F32)],
        ),
        out_shape=[jax.ShapeDtypeStruct(cut, F32)] + [jax.ShapeDtypeStruct(cut, BF16)] * 3,
        compiler_params=params(8),
        cost_estimate=LITTLE,
        name="ring_total",
    )(me, later, below0, above0, below1, above1)


def after(values, *deps):
    return lax.optimization_barrier((values, deps))[0]


def on_device(tokens, picks, counts, score, w_in, w_out, cotan):
    routed = picks.shape[0]
    n_tok = tokens.shape[0]

    own_mine, me = take_rows(tokens, picks, counts, score, cotan)
    w_in, w_out = hold(*after((w_in, w_out), own_mine))
    near_mine = move_lane(own_mine, 1)
    own_other = swap_core(own_mine)
    own_packs = [own_mine, own_other]
    own = hidden_units(own_packs, w_in, w_out)

    near_other = move_lane(own_other, 1)
    own_terms = row_terms(own[0], own[1], w_in, w_out, routed, 1)
    own_got = swap_core(own_terms[1])
    near_mine = after(near_mine, own)
    far_mine = move_lane(near_mine, 1)
    near_packs = [near_mine, near_other, swap_core(near_mine), swap_core(near_other)]
    near_packs, own_got = after((near_packs, own_got), own)
    near = hidden_units(near_packs, w_in, w_out)

    near_terms = row_terms(near[0], near[1], w_in, w_out, routed, 3)
    far_mine = after(far_mine, near_terms)
    far_packs = [far_mine, swap_core(far_mine)]
    far = hidden_units(far_packs, w_in, w_out)
    last_terms = row_terms(far[0], far[1], w_in, w_out, routed, 3, near_terms)
    last_got = swap_core(last_terms[1])

    all_packs = own_packs + near_packs + far_packs
    hidden, dpre, turned = ([u[i] for u in (own, near, far)] for i in range(3))
    all_packs, dpre = after((all_packs, dpre), last_terms)
    in_up, in_down = in_blocks(me, all_packs, dpre, first_step, True)
    in_below, in_above = move_x(in_up, 1), move_x(in_down, -1)

    last_got = after(last_got, in_up, in_down)
    to_far = (last_terms[0][2].astype(F32) + last_got[2].astype(F32)).astype(BF16)
    z_far = move_lane(to_far, -1)

    hidden, turned = after((hidden, turned), to_far)
    out_up, out_down = out_blocks(me, hidden, turned, first_step, True)
    out_below, out_above = move_y(out_up, 1), move_y(out_down, -1)
    all_packs, dpre = after((all_packs, dpre), out_up, out_down)
    in_later = in_blocks(me, all_packs, dpre, later_step, False)[0]
    z_far = after(z_far, in_later)
    passed = jnp.pad(z_far.astype(F32)[None], ((0, 1), (0, 0), (0, 0), (0, 0)))
    to_near = (last_terms[0][:2].astype(F32) + last_got[:2].astype(F32) + passed).astype(BF16)
    z_near = move_lane(to_near, -1)
    hidden, turned = after((hidden, turned), to_near)
    out_later = out_blocks(me, hidden, turned, later_step, False)[0]

    def second_hop(later, from_below, from_above, move):
        up = (later[0].astype(F32) + from_below[0].astype(F32)).astype(BF16)
        down = (later[1].astype(F32) + from_above[0].astype(F32)).astype(BF16)
        return move(up, 1), move(down, -1), up, down

    in_below, in_above, out_below, out_above = after((in_below, in_above, out_below, out_above), out_later)
    in_hops = second_hop(in_later, in_below, in_above, move_x)
    out_hops = second_hop(out_later, out_below, out_above, move_y)
    in_hops, out_hops = lax.optimization_barrier((in_hops[:2], out_hops[:2]))
    z_near = after(z_near, in_hops, out_hops)
    z_other = swap_core(z_near[1])

    def second_stage(total, move):
        keep, following, previous, far = total
        return keep, move(far, 2), move(following, 1), move(previous, -1)

    def add_up(parts):
        return parts[0] + parts[1].astype(F32) + parts[2].astype(F32) + parts[3].astype(F32)

    in_total = ring_total(me, in_later, in_hops[0], in_above, in_below, in_hops[1], True)
    out_total = ring_total(me, out_later, out_hops[0], out_above, out_below, out_hops[1], False)
    in_total, out_total = after((in_total, out_total), z_other)
    in_parts = second_stage(in_total, move_y)
    out_parts = second_stage(out_total, move_x)

    back = (
        own_terms[0][0].astype(F32) + own_got[0].astype(F32) + z_near[0].astype(F32) + z_other.astype(F32)
    ).astype(BF16)
    ffn = back[0].astype(F32)
    heavy = (score[:, None] * ffn).astype(BF16)
    grad_score = jnp.sum(cotan.astype(F32) * ffn, axis=1)
    place = picks[:, None] == jnp.arange(n_tok, dtype=jnp.int32)[None, :]
    grad_x = dot(place.astype(BF16), back[1], ((0,), (0,))).astype(BF16)
    in_parts, out_parts = after((in_parts, out_parts), heavy, grad_x)
    grad_in = add_up(in_parts)
    grad_out = add_up(out_parts)
    return (heavy, grad_x, grad_score, grad_in, grad_out)


def solution(mesh):
    placed = (
        P(("ctx", "head"), None),
        P(("ctx", "head")),
        P(("ctx", "head")),
        P(("ctx", "head")),
        P(None, "head"),
        P("head", None),
        P(("ctx", "head"), None),
    )
    return jax.shard_map(
        on_device,
        mesh=mesh,
        in_specs=placed,
        out_specs=(
            P(("ctx", "head"), None),
            P(("ctx", "head"), None),
            P(("ctx", "head")),
            P("ctx", "head"),
            P("head", "ctx"),
        ),
        check_vma=False,
    )
```

```python
import functools

import jax
import jax.numpy as jnp
from jax import lax
from jax.experimental import pallas as pl
from jax.experimental.pallas import tpu as pltpu
from jax.sharding import PartitionSpec as P

F32 = jnp.float32
BF16 = jnp.bfloat16
SIDE = 4
MIB = 1024 * 1024
LITTLE = pl.CostEstimate(flops=1, bytes_accessed=1, transcendentals=0)


def gelu_parts(u):
    c = 0.7978845608
    t = jnp.tanh(c * (u + 0.044715 * u * u * u))
    value = 0.5 * u * (1.0 + t)
    slope = 0.5 * (1.0 + t) + 0.5 * u * (1.0 - t * t) * c * (1.0 + 3.0 * 0.044715 * u * u)
    return (value, slope)


def move_x(v, by):
    perm = [(x * SIDE + y, ((x + by) % SIDE) * SIDE + y) for x in range(SIDE) for y in range(SIDE)]
    return lax.ppermute(v, "ctx", perm)


def move_y(v, by):
    perm = [(x * SIDE + y, x * SIDE + (y + by) % SIDE) for x in range(SIDE) for y in range(SIDE)]
    return lax.ppermute(v, "ctx", perm)


def move_lane(v, by):
    perm = [(z * 2 + c, ((z + (by if c == 0 else -by)) % SIDE) * 2 + c) for z in range(SIDE) for c in range(2)]
    return lax.ppermute(v, "head", perm)


def swap_core(v):
    return lax.ppermute(v, "head", [(i, i ^ 1) for i in range(2 * SIDE)])


def dot(a, b, dims):
    return lax.dot_general(a, b, ((dims[0], dims[1]), ((), ())), preferred_element_type=F32)


def params(mib):
    return pltpu.CompilerParams(vmem_limit_bytes=mib * MIB)


def whole(a):
    return pl.BlockSpec(a.shape, lambda *_: (0,) * a.ndim)


def take_rows(tokens, picks, counts, score, cotan):
    routed = picks.shape[0]
    n_tok, width = tokens.shape

    def body(counts_ref, tokens_ref, picks_ref, score_ref, cotan_ref, out_ref, me_ref):
        me_ref[0] = lax.axis_index("ctx").astype(jnp.int32)
        me_ref[1] = lax.axis_index("head").astype(jnp.int32)
        places = lax.broadcasted_iota(jnp.int32, (n_tok, routed), 0)
        slots = lax.broadcasted_iota(jnp.int32, (n_tok, routed), 1)
        hit = (places == picks_ref[...]) & (slots < counts_ref[0])
        one_hot = jnp.where(hit, 1.0, 0.0).astype(BF16)
        out_ref[0] = dot(one_hot, tokens_ref[...], ((0,), (0,))).astype(BF16)
        across = lax.broadcasted_iota(jnp.int32, (routed, routed), 0)
        along = lax.broadcasted_iota(jnp.int32, (routed, routed), 1)
        kept = (across == along) & (along < counts_ref[0])
        factor = jnp.sum(jnp.where(kept, score_ref[...], 0.0), axis=1, keepdims=True)
        out_ref[1] = (factor * cotan_ref[...].astype(F32)).astype(BF16)

    return pl.pallas_call(
        body,
        grid_spec=pltpu.PrefetchScalarGridSpec(
            num_scalar_prefetch=1,
            grid=(1,),
            in_specs=[
                whole(tokens),
                pl.BlockSpec((1, routed), lambda i, c: (0, 0)),
                pl.BlockSpec((1, routed), lambda i, c: (0, 0)),
                whole(cotan),
            ],
            out_specs=[
                pl.BlockSpec((2, routed, width), lambda i, c: (0, 0, 0)),
                pl.BlockSpec(memory_space=pltpu.SMEM),
            ],
        ),
        out_shape=[jax.ShapeDtypeStruct((2, routed, width), BF16), jax.ShapeDtypeStruct((2,), jnp.int32)],
        compiler_params=params(60),
        cost_estimate=LITTLE,
        name="take_rows",
    )(counts, tokens, picks[None, :], score[None, :], cotan)


def hidden_units(packs, w_in, w_out):
    halves = [(i, h) for i, p in enumerate(packs) for h in range(len(p))]
    at = {p: k for k, p in enumerate(halves)}
    where_r = [at[(i, 0)] for i in range(len(packs))]
    where_d = [at[(i, len(p) - 1)] for i, p in enumerate(packs)]
    flat = [a for p in packs for a in p]
    n = len(packs)
    _, piece, width = flat[0].shape
    count = n * piece
    hid = w_in.shape[1]
    tile = hid // SIDE
    quarter = width // SIDE
    strip = quarter // SIDE

    def body(*refs):
        last = [refs[k].shape[0] - 1 for k in where_d]
        r = jnp.concatenate([refs[k][0] for k in where_r], axis=0)
        d = jnp.concatenate([refs[k][i] for k, i in zip(where_d, last)], axis=0)
        win_ref, wout_ref, hidden_ref, dpre_ref, turned_ref = refs[len(flat) :]
        pre = dot(r, win_ref[...], ((1,), (0,)))
        dhid = dot(d, wout_ref[...], ((1,), (1,)))
        value, slope = gelu_parts(pre)
        hidden_ref[...] = value.astype(BF16)
        dpre_ref[...] = (dhid * slope).astype(BF16)
        y = pl.program_id(0)
        for x in range(SIDE):
            at = pl.multiple_of(x * quarter + y * strip, strip)
            for k in range(n):
                turned_ref[pl.ds(k * piece, piece), pl.ds(x * strip, strip)] = refs[where_d[k]][
                    last[k], :, pl.ds(at, strip)
                ]

    return pl.pallas_call(
        body,
        grid=(SIDE,),
        in_specs=[whole(a) for a in flat]
        + [
            pl.BlockSpec((width, tile), lambda j: (0, j)),
            pl.BlockSpec((tile, width), lambda j: (j, 0)),
        ],
        out_specs=[
            pl.BlockSpec((count, tile), lambda j: (0, j)),
            pl.BlockSpec((count, tile), lambda j: (0, j)),
            pl.BlockSpec((count, quarter), lambda j: (0, j)),
        ],
        out_shape=[
            jax.ShapeDtypeStruct((count, hid), BF16),
            jax.ShapeDtypeStruct((count, hid), BF16),
            jax.ShapeDtypeStruct((count, width), BF16),
        ],
        compiler_params=params(4 + count // 64),
        cost_estimate=LITTLE,
        name="hidden_units",
    )(*flat, held(w_in), held(w_out))


def hold(w_in, w_out):
    def body(win_ref, wout_ref, win_out, wout_out, sems):
        copies = [
            pltpu.make_async_copy(win_ref, win_out, sems.at[0]),
            pltpu.make_async_copy(wout_ref, wout_out, sems.at[1]),
        ]
        for copy in copies:
            copy.start()
        for copy in copies:
            copy.wait()

    return pl.pallas_call(
        body,
        in_specs=[pl.BlockSpec(memory_space=pl.ANY)] * 2,
        out_specs=[pl.BlockSpec(memory_space=pltpu.VMEM)] * 2,
        out_shape=[pltpu.VMEM(w.shape, w.dtype) for w in (w_in, w_out)],
        scratch_shapes=[pltpu.SemaphoreType.DMA((2,))],
        compiler_params=params(4),
        cost_estimate=LITTLE,
        name="hold_weights",
    )(pltpu.with_memory_space_constraint(w_in, pltpu.HBM), pltpu.with_memory_space_constraint(w_out, pltpu.HBM))


def held(w):
    return pltpu.with_memory_space_constraint(w, pltpu.VMEM)


def row_terms(hidden, dpre, w_in, w_out, piece, groups, first=0, held_terms=()):
    count, hid = hidden.shape
    width = w_in.shape[0]
    n = count // (2 * piece)
    tile = width // SIDE

    def body(hidden_ref, dpre_ref, win_ref, wout_ref, *refs):
        outs = refs[len(held_terms) :]
        ffn = dot(hidden_ref[...], wout_ref[...], ((1,), (0,))).astype(BF16)
        dx = dot(dpre_ref[...], win_ref[...], ((1,), (1,))).astype(BF16)
        for h in range(2):
            for k in range(n):
                for s, v in enumerate((ffn, dx)):
                    outs[h][k, s] = v[(h * n + k) * piece : (h * n + k + 1) * piece]

    return pl.pallas_call(
        body,
        grid=(SIDE,),
        in_specs=[
            whole(hidden),
            whole(dpre),
            pl.BlockSpec((tile, hid), lambda j: (j, 0)),
            pl.BlockSpec((hid, tile), lambda j: (0, j)),
        ]
        + [pl.BlockSpec(memory_space=pl.ANY)] * len(held_terms),
        out_specs=[pl.BlockSpec((n, 2, piece, tile), lambda j: (first, 0, 0, j))] * 2,
        out_shape=[jax.ShapeDtypeStruct((groups, 2, piece, width), BF16)] * 2,
        input_output_aliases={4 + i: i for i in range(len(held_terms))},
        compiler_params=params(6 + count // 64),
        cost_estimate=LITTLE,
        name="row_terms",
    )(hidden, dpre, held(w_in), held(w_out), *held_terms)


def first_step(i):
    place = jnp.where(i < 2, 2, jnp.where(i == 2, 1, 3))
    half = jnp.where((i == 1) | (i == 2), 1, 0)
    return place, half


def later_step(i):
    place = jnp.where(i >= 2, 0, jnp.where(i == 0, 1, 3))
    half = jnp.where((i == 1) | (i == 3), 1, 0)
    return place, half


def in_blocks(me, packs, dpre, order, split):
    n = len(packs)
    _, piece, width = packs[0].shape
    hid = dpre[0].shape[1]
    size = width // (2 * SIDE)

    def body(me_ref, *refs):
        i = pl.program_id(0)
        r = jnp.concatenate([ref[0] for ref in refs[:n]], axis=0)
        d = jnp.concatenate([ref[...] for ref in refs[n : n + len(dpre)]], axis=0)
        term = dot(r, d, ((0,), (0,))).astype(BF16)
        outs = refs[n + len(dpre) :]
        if split:
            for s in range(2):

                @pl.when(lax.rem(i, 2) == s)
                def _():
                    outs[s][0] = term

        else:
            outs[0][0] = term

    def columns(i, me_ref):
        place, half = order(i)
        return (0, 0, 2 * lax.rem(me_ref[0] // SIDE + place, SIDE) + half)

    return blocks_call(body, me, [pl.BlockSpec((1, piece, size), columns)] * n + [whole(a) for a in dpre],
                       packs + dpre, (size, hid), split, n * piece)


def out_blocks(me, hidden, turned, order, split):
    count = sum(a.shape[0] for a in hidden)
    hid = hidden[0].shape[1]
    quarter = turned[0].shape[1] // SIDE

    def body(me_ref, *refs):
        i = pl.program_id(0)
        n = len(hidden)
        h = jnp.concatenate([ref[...] for ref in refs[:n]], axis=0)
        d = jnp.concatenate([ref[...] for ref in refs[n : 2 * n]], axis=0)
        term = dot(h, d, ((0,), (0,))).astype(BF16)
        outs = refs[2 * n :]
        if split:
            for s in range(2):

                @pl.when(lax.rem(i, 2) == s)
                def _():
                    outs[s][0] = term

        else:
            outs[0][0] = term

    def units(i, me_ref):
        return (0, order(i)[1])

    def columns(i, me_ref):
        return (0, lax.rem(lax.rem(me_ref[0], SIDE) + order(i)[0], SIDE))

    specs = [pl.BlockSpec((a.shape[0], hid // 2), units) for a in hidden]
    specs += [pl.BlockSpec((a.shape[0], quarter), columns) for a in turned]
    return blocks_call(body, me, specs, hidden + turned, (hid // 2, quarter), split, count)


def blocks_call(body, me, specs, args, block, split, count):
    if split:
        shapes = [jax.ShapeDtypeStruct((2,) + block, BF16)] * 2
        outs = [pl.BlockSpec((1,) + block, lambda i, me_ref: (i // 2, 0, 0))] * 2
    else:
        shapes = [jax.ShapeDtypeStruct((4,) + block, BF16)]
        outs = [pl.BlockSpec((1,) + block, lambda i, me_ref: (i, 0, 0))]
    return pl.pallas_call(
        body,
        grid_spec=pltpu.PrefetchScalarGridSpec(
            num_scalar_prefetch=1, grid=(4,), in_specs=specs, out_specs=outs
        ),
        out_shape=shapes,
        compiler_params=params(8),
        cost_estimate=LITTLE,
        name="weight_blocks",
    )(me, *args)


def ring_total(me, later, below0, above0, below1, above1, rowwise):
    block = later.shape[1:]
    if rowwise:
        cut = (2 * block[0] // SIDE, block[1])
    else:
        cut = (2 * block[0], block[1] // SIDE)

    def body(me_ref, later_ref, b0, a0, b1, a1, keep_ref, next_ref, prev_ref, far_ref, sum_ref):
        half = block[0]
        sum_ref[pl.ds(0, half), :] = later_ref[0].astype(F32) + b0[...].astype(F32) + a0[0].astype(F32)
        sum_ref[pl.ds(half, half), :] = later_ref[1].astype(F32) + b1[0].astype(F32) + a1[...].astype(F32)
        if rowwise:
            at = lax.rem(me_ref[0], SIDE)
        else:
            at = me_ref[0] // SIDE
        for k, ref in ((0, keep_ref), (1, next_ref), (3, prev_ref), (2, far_ref)):
            to = lax.rem(at + k, SIDE)
            if rowwise:
                v = sum_ref[pl.ds(pl.multiple_of(to * cut[0], cut[0]), cut[0]), :]
            else:
                v = sum_ref[:, pl.ds(pl.multiple_of(to * cut[1], cut[1]), cut[1])]
            ref[...] = v.astype(ref.dtype)

    second = pl.BlockSpec((2,) + block, lambda i, me_ref: (1, 0, 0))
    one = pl.BlockSpec(block, lambda i, me_ref: (0, 0))
    tail = pl.BlockSpec((1,) + block, lambda i, me_ref: (1, 0, 0))
    out = pl.BlockSpec(cut, lambda i, me_ref: (0, 0))
    return pl.pallas_call(
        body,
        grid_spec=pltpu.PrefetchScalarGridSpec(
            num_scalar_prefetch=1,
            grid=(1,),
            in_specs=[second, one, tail, tail, one],
            out_specs=[out] * 4,
            scratch_shapes=[pltpu.VMEM((2 * block[0], block[1]), F32)],
        ),
        out_shape=[jax.ShapeDtypeStruct(cut, F32)] + [jax.ShapeDtypeStruct(cut, BF16)] * 3,
        compiler_params=params(8),
        cost_estimate=LITTLE,
        name="ring_total",
    )(me, later, below0, above0, below1, above1)


def after(values, *deps):
    return lax.optimization_barrier((values, deps))[0]


def on_device(tokens, picks, counts, score, w_in, w_out, cotan):
    routed = picks.shape[0]
    n_tok = tokens.shape[0]

    own_mine, me = take_rows(tokens, picks, counts, score, cotan)
    w_in, w_out = hold(*after((w_in, w_out), own_mine))
    near_mine = move_lane(own_mine, 1)
    own_other = swap_core(own_mine)
    own = hidden_units([[own_mine], [own_other]], w_in, w_out)

    near_other = move_lane(own_other, 1)
    near_mine = after(near_mine, own)
    far_mine = move_lane(near_mine, 1)
    swapped_mine = [swap_core(near_mine[:1]), swap_core(near_mine[1:])]
    own_terms = row_terms(own[0], own[1], w_in, w_out, routed, 1)
    own_got = swap_core(own_terms[1])
    near_mine, swapped_mine = after((near_mine, swapped_mine), own_terms)
    near = hidden_units([[near_mine], swapped_mine], w_in, w_out)
    near_terms = row_terms(near[0], near[1], w_in, w_out, routed, 3)

    near_other = after(near_other, near)
    swapped_other = [swap_core(near_other[:1]), swap_core(near_other[1:])]
    swapped_other, own_got = after((swapped_other, own_got), near_terms)
    other = hidden_units([[near_other], swapped_other], w_in, w_out)
    near_terms = row_terms(other[0], other[1], w_in, w_out, routed, 3, 1, near_terms)

    far_mine = after(far_mine, other)
    far_packs = after([far_mine, swap_core(far_mine)], near_terms)
    far = hidden_units([[p] for p in far_packs], w_in, w_out)
    last_terms = row_terms(far[0], far[1], w_in, w_out, routed, 3, 2, near_terms)
    last_got = swap_core(last_terms[1])

    all_packs = [own_mine, own_other, near_mine, swapped_mine[0], near_other, swapped_other[0]] + far_packs
    hidden, dpre, turned = ([u[i] for u in (own, near, other, far)] for i in range(3))
    all_packs, dpre = after((all_packs, dpre), last_terms)
    in_up, in_down = in_blocks(me, all_packs, dpre, first_step, True)
    in_below, in_above = move_x(in_up, 1), move_x(in_down, -1)

    hidden, turned = after((hidden, turned), in_up, in_down)
    out_up, out_down = out_blocks(me, hidden, turned, first_step, True)
    out_below, out_above = move_y(out_up, 1), move_y(out_down, -1)

    last_got = after(last_got, out_up, out_down)
    to_far = (last_terms[0][2].astype(F32) + last_got[2].astype(F32)).astype(BF16)
    z_far = move_lane(to_far, -1)
    all_packs, dpre = after((all_packs, dpre), to_far)
    in_later = in_blocks(me, all_packs, dpre, later_step, False)[0]
    z_far = after(z_far, in_later)
    passed = jnp.pad(z_far.astype(F32)[None], ((0, 1), (0, 0), (0, 0), (0, 0)))
    to_near = (last_terms[0][:2].astype(F32) + last_got[:2].astype(F32) + passed).astype(BF16)
    z_near = move_lane(to_near, -1)
    hidden, turned = after((hidden, turned), to_near)
    out_later = out_blocks(me, hidden, turned, later_step, False)[0]

    def second_hop(later, from_below, from_above, move):
        up = (later[0].astype(F32) + from_below[0].astype(F32)).astype(BF16)
        down = (later[1].astype(F32) + from_above[0].astype(F32)).astype(BF16)
        return move(up, 1), move(down, -1), up, down

    in_below, in_above, out_below, out_above = after((in_below, in_above, out_below, out_above), out_later)
    in_hops = second_hop(in_later, in_below, in_above, move_x)
    out_hops = second_hop(out_later, out_below, out_above, move_y)
    in_hops, out_hops = lax.optimization_barrier((in_hops[:2], out_hops[:2]))
    z_near = after(z_near, in_hops, out_hops)
    z_other = swap_core(z_near[1])

    def second_stage(total, move):
        keep, following, previous, far = total
        return keep, move(far, 2), move(following, 1), move(previous, -1)

    def add_up(parts):
        return parts[0] + parts[1].astype(F32) + parts[2].astype(F32) + parts[3].astype(F32)

    in_total = ring_total(me, in_later, in_hops[0], in_above, in_below, in_hops[1], True)
    out_total = ring_total(me, out_later, out_hops[0], out_above, out_below, out_hops[1], False)
    in_total, out_total = after((in_total, out_total), z_other)
    in_parts = second_stage(in_total, move_y)
    out_parts = second_stage(out_total, move_x)

    back = (
        own_terms[0][0].astype(F32) + own_got[0].astype(F32) + z_near[0].astype(F32) + z_other.astype(F32)
    ).astype(BF16)
    ffn = back[0].astype(F32)
    heavy = (score[:, None] * ffn).astype(BF16)
    grad_score = jnp.sum(cotan.astype(F32) * ffn, axis=1)
    place = picks[:, None] == jnp.arange(n_tok, dtype=jnp.int32)[None, :]
    grad_x = dot(place.astype(BF16), back[1], ((0,), (0,))).astype(BF16)
    in_parts, out_parts = after((in_parts, out_parts), heavy, grad_x)
    grad_in = add_up(in_parts)
    grad_out = add_up(out_parts)
    return (heavy, grad_x, grad_score, grad_in, grad_out)


def solution(mesh):
    placed = (
        P(("ctx", "head"), None),
        P(("ctx", "head")),
        P(("ctx", "head")),
        P(("ctx", "head")),
        P(None, "head"),
        P("head", None),
        P(("ctx", "head"), None),
    )
    return jax.shard_map(
        on_device,
        mesh=mesh,
        in_specs=placed,
        out_specs=(
            P(("ctx", "head"), None),
            P(("ctx", "head"), None),
            P(("ctx", "head")),
            P("ctx", "head"),
            P("head", "ctx"),
        ),
        check_vma=False,
    )
```

```python
import functools

import jax
import jax.numpy as jnp
from jax import lax
from jax.experimental import pallas as pl
from jax.experimental.pallas import tpu as pltpu
from jax.sharding import PartitionSpec as P

F32 = jnp.float32
BF16 = jnp.bfloat16
SIDE = 4
MIB = 1024 * 1024
LITTLE = pl.CostEstimate(flops=1, bytes_accessed=1, transcendentals=0)


def gelu_parts(u):
    c = 0.7978845608
    t = jnp.tanh(c * (u + 0.044715 * u * u * u))
    value = 0.5 * u * (1.0 + t)
    slope = 0.5 * (1.0 + t) + 0.5 * u * (1.0 - t * t) * c * (1.0 + 3.0 * 0.044715 * u * u)
    return (value, slope)


def move_x(v, by):
    perm = [(x * SIDE + y, ((x + by) % SIDE) * SIDE + y) for x in range(SIDE) for y in range(SIDE)]
    return lax.ppermute(v, "ctx", perm)


def move_y(v, by):
    perm = [(x * SIDE + y, x * SIDE + (y + by) % SIDE) for x in range(SIDE) for y in range(SIDE)]
    return lax.ppermute(v, "ctx", perm)


def move_lane(v, by):
    perm = [(z * 2 + c, ((z + (by if c == 0 else -by)) % SIDE) * 2 + c) for z in range(SIDE) for c in range(2)]
    return lax.ppermute(v, "head", perm)


def swap_core(v):
    return lax.ppermute(v, "head", [(i, i ^ 1) for i in range(2 * SIDE)])


def dot(a, b, dims):
    return lax.dot_general(a, b, ((dims[0], dims[1]), ((), ())), preferred_element_type=F32)


def params(mib):
    return pltpu.CompilerParams(vmem_limit_bytes=mib * MIB)


def whole(a):
    return pl.BlockSpec(a.shape, lambda *_: (0,) * a.ndim)


def take_rows(tokens, picks, counts, score, cotan):
    routed = picks.shape[0]
    n_tok, width = tokens.shape

    def body(counts_ref, tokens_ref, picks_ref, score_ref, cotan_ref, out_ref, me_ref):
        me_ref[0] = lax.axis_index("ctx").astype(jnp.int32)
        me_ref[1] = lax.axis_index("head").astype(jnp.int32)
        places = lax.broadcasted_iota(jnp.int32, (n_tok, routed), 0)
        slots = lax.broadcasted_iota(jnp.int32, (n_tok, routed), 1)
        hit = (places == picks_ref[...]) & (slots < counts_ref[0])
        one_hot = jnp.where(hit, 1.0, 0.0).astype(BF16)
        out_ref[0] = dot(one_hot, tokens_ref[...], ((0,), (0,))).astype(BF16)
        across = lax.broadcasted_iota(jnp.int32, (routed, routed), 0)
        along = lax.broadcasted_iota(jnp.int32, (routed, routed), 1)
        kept = (across == along) & (along < counts_ref[0])
        factor = jnp.sum(jnp.where(kept, score_ref[...], 0.0), axis=1, keepdims=True)
        out_ref[1] = (factor * cotan_ref[...].astype(F32)).astype(BF16)

    return pl.pallas_call(
        body,
        grid_spec=pltpu.PrefetchScalarGridSpec(
            num_scalar_prefetch=1,
            grid=(1,),
            in_specs=[
                whole(tokens),
                pl.BlockSpec((1, routed), lambda i, c: (0, 0)),
                pl.BlockSpec((1, routed), lambda i, c: (0, 0)),
                whole(cotan),
            ],
            out_specs=[
                pl.BlockSpec((2, routed, width), lambda i, c: (0, 0, 0)),
                pl.BlockSpec(memory_space=pltpu.SMEM),
            ],
        ),
        out_shape=[jax.ShapeDtypeStruct((2, routed, width), BF16), jax.ShapeDtypeStruct((2,), jnp.int32)],
        compiler_params=params(60),
        cost_estimate=LITTLE,
        name="take_rows",
    )(counts, tokens, picks[None, :], score[None, :], cotan)


IN_VMEM = pl.BlockSpec(memory_space=pltpu.VMEM)
IN_SMEM = pl.BlockSpec(memory_space=pltpu.SMEM)


def held(a):
    return pltpu.with_memory_space_constraint(a, pltpu.VMEM)


def on_held(body, arrays, shapes, name, me=None, spare=(), aliases={}):
    first = [] if me is None else [me]
    return pl.pallas_call(
        body,
        in_specs=[IN_SMEM] * len(first) + [IN_VMEM] * len(arrays) + [pl.BlockSpec(memory_space=pl.ANY)] * len(spare),
        out_specs=[IN_VMEM] * len(shapes),
        out_shape=[pltpu.VMEM(shape, dtype) for shape, dtype in shapes],
        input_output_aliases=aliases,
        compiler_params=params(12),
        cost_estimate=LITTLE,
        name=name,
    )(*first, *[held(a) for a in arrays], *[held(a) for a in spare])


def hidden_units(packs, w_in, w_out):
    halves = [(i, h) for i, p in enumerate(packs) for h in range(len(p))]
    at = {p: k for k, p in enumerate(halves)}
    where_r = [at[(i, 0)] for i in range(len(packs))]
    where_d = [at[(i, len(p) - 1)] for i, p in enumerate(packs)]
    flat = [a for p in packs for a in p]
    n = len(packs)
    _, piece, width = flat[0].shape
    count = n * piece
    hid = w_in.shape[1]
    tile = hid // SIDE
    quarter = width // SIDE
    strip = quarter // SIDE

    def body(*refs):
        last = [refs[k].shape[0] - 1 for k in where_d]
        r = jnp.concatenate([refs[k][0] for k in where_r], axis=0)
        d = jnp.concatenate([refs[k][i] for k, i in zip(where_d, last)], axis=0)
        win_ref, wout_ref, hidden_ref, dpre_ref, turned_ref = refs[len(flat) :]
        for j in range(SIDE):
            cols = pl.ds(j * tile, tile)
            pre = dot(r, win_ref[:, cols], ((1,), (0,)))
            dhid = dot(d, wout_ref[cols, :], ((1,), (1,)))
            value, slope = gelu_parts(pre)
            hidden_ref[:, cols] = value.astype(BF16)
            dpre_ref[:, cols] = (dhid * slope).astype(BF16)
        for y in range(SIDE):
            for x in range(SIDE):
                to = pl.ds(y * quarter + x * strip, strip)
                for k in range(n):
                    turned_ref[pl.ds(k * piece, piece), to] = refs[where_d[k]][
                        last[k], :, pl.ds(x * quarter + y * strip, strip)
                    ]

    shapes = [((count, hid), BF16), ((count, hid), BF16), ((count, width), BF16)]
    return on_held(body, flat + [w_in, w_out], shapes, "hidden_units")


def hold(w_in, w_out):
    def body(win_ref, wout_ref, win_out, wout_out, sems):
        copies = [
            pltpu.make_async_copy(win_ref, win_out, sems.at[0]),
            pltpu.make_async_copy(wout_ref, wout_out, sems.at[1]),
        ]
        for copy in copies:
            copy.start()
        for copy in copies:
            copy.wait()

    return pl.pallas_call(
        body,
        in_specs=[pl.BlockSpec(memory_space=pl.ANY)] * 2,
        out_specs=[pl.BlockSpec(memory_space=pltpu.VMEM)] * 2,
        out_shape=[pltpu.VMEM(w.shape, w.dtype) for w in (w_in, w_out)],
        scratch_shapes=[pltpu.SemaphoreType.DMA((2,))],
        compiler_params=params(4),
        cost_estimate=LITTLE,
        name="hold_weights",
    )(pltpu.with_memory_space_constraint(w_in, pltpu.HBM), pltpu.with_memory_space_constraint(w_out, pltpu.HBM))


def row_terms(hidden, dpre, w_in, w_out, piece, groups, first=0, held_terms=()):
    count, hid = hidden.shape
    width = w_in.shape[0]
    n = count // (2 * piece)
    tile = width // SIDE

    def body(hidden_ref, dpre_ref, win_ref, wout_ref, *refs):
        outs = refs[len(held_terms) :]
        for j in range(SIDE):
            cols = pl.ds(j * tile, tile)
            ffn = dot(hidden_ref[...], wout_ref[:, cols], ((1,), (0,))).astype(BF16)
            dx = dot(dpre_ref[...], win_ref[cols, :], ((1,), (1,))).astype(BF16)
            for h in range(2):
                for k in range(n):
                    for s, v in enumerate((ffn, dx)):
                        outs[h][first + k, s, :, cols] = v[(h * n + k) * piece : (h * n + k + 1) * piece]

    shapes = [((groups, 2, piece, width), BF16)] * 2
    aliases = {4 + i: i for i in range(len(held_terms))}
    return on_held(body, [hidden, dpre, w_in, w_out], shapes, "row_terms", spare=held_terms, aliases=aliases)


FIRST_STEP = ((2, 0), (2, 1), (1, 1), (3, 0))
LATER_STEP = ((1, 0), (3, 1), (0, 0), (0, 1))


def store_block(outs, i, term):
    if len(outs) == 2:
        outs[i % 2][i // 2] = term.astype(BF16)
    else:
        outs[0][i] = term.astype(BF16)


def block_shapes(steps, block):
    return [((2,) + block, BF16)] * 2 if steps is FIRST_STEP else [((len(steps),) + block, BF16)]


def in_blocks(me, packs, dpre, steps):
    n = len(packs)
    _, piece, width = packs[0].shape
    hid = dpre[0].shape[1]
    size = width // (2 * SIDE)
    each = n // len(dpre)

    def body(me_ref, *refs):
        for i, (place, half) in enumerate(steps):
            to = 2 * lax.rem(me_ref[0] // SIDE + place, SIDE) + half
            cols = pl.ds(pl.multiple_of(to * size, size), size)
            term = None
            for c in range(len(dpre)):
                r = jnp.concatenate([ref[0, :, cols] for ref in refs[c * each : (c + 1) * each]], axis=0)
                part = dot(r, refs[n + c][...], ((0,), (0,)))
                term = part if term is None else term + part
            store_block(refs[n + len(dpre) :], i, term)

    return on_held(body, packs + dpre, block_shapes(steps, (size, hid)), "in_blocks", me)


def out_blocks(me, hidden, turned, steps):
    n = len(hidden)
    hid = hidden[0].shape[1]
    quarter = turned[0].shape[1] // SIDE

    def body(me_ref, *refs):
        for i, (place, half) in enumerate(steps):
            to = lax.rem(lax.rem(me_ref[0], SIDE) + place, SIDE)
            cols = pl.ds(pl.multiple_of(to * quarter, quarter), quarter)
            term = None
            for c in range(n):
                h = refs[c][:, pl.ds(half * (hid // 2), hid // 2)]
                part = dot(h, refs[n + c][:, cols], ((0,), (0,)))
                term = part if term is None else term + part
            store_block(refs[2 * n :], i, term)

    return on_held(body, hidden + turned, block_shapes(steps, (hid // 2, quarter)), "out_blocks", me)


def ring_total(me, later, below0, above0, below1, above1, rowwise):
    block = later.shape[1:]
    if rowwise:
        cut = (2 * block[0] // SIDE, block[1])
    else:
        cut = (2 * block[0], block[1] // SIDE)

    def body(me_ref, later_ref, b0, a0, b1, a1, keep_ref, next_ref, prev_ref, far_ref, sum_ref):
        half = block[0]
        sum_ref[pl.ds(0, half), :] = later_ref[2].astype(F32) + b0[...].astype(F32) + a0[1].astype(F32)
        sum_ref[pl.ds(half, half), :] = later_ref[3].astype(F32) + b1[1].astype(F32) + a1[...].astype(F32)
        if rowwise:
            at = lax.rem(me_ref[0], SIDE)
        else:
            at = me_ref[0] // SIDE
        for k, ref in ((0, keep_ref), (1, next_ref), (3, prev_ref), (2, far_ref)):
            to = lax.rem(at + k, SIDE)
            if rowwise:
                v = sum_ref[pl.ds(pl.multiple_of(to * cut[0], cut[0]), cut[0]), :]
            else:
                v = sum_ref[:, pl.ds(pl.multiple_of(to * cut[1], cut[1]), cut[1])]
            ref[...] = v.astype(ref.dtype)

    return pl.pallas_call(
        body,
        in_specs=[IN_SMEM] + [IN_VMEM] * 5,
        out_specs=[IN_VMEM] * 4,
        out_shape=[pltpu.VMEM(cut, F32)] + [pltpu.VMEM(cut, BF16)] * 3,
        scratch_shapes=[pltpu.VMEM((2 * block[0], block[1]), F32)],
        compiler_params=params(12),
        cost_estimate=LITTLE,
        name="ring_total",
    )(me, *[held(a) for a in (later, below0, above0, below1, above1)])


def add_up(*groups):
    flat = [a for g in groups for a in g]

    def body(*refs):
        at = 0
        for g, out_ref in zip(groups, refs[len(flat) :]):
            total = refs[at][...].astype(F32)
            for ref in refs[at + 1 : at + len(g)]:
                total += ref[...].astype(F32)
            out_ref[...] = total
            at += len(g)

    return pl.pallas_call(
        body,
        grid=(1,),
        in_specs=[whole(a) for a in flat],
        out_specs=[whole(g[0]) for g in groups],
        out_shape=[jax.ShapeDtypeStruct(g[0].shape, F32) for g in groups],
        compiler_params=params(10),
        cost_estimate=LITTLE,
        name="add_up",
    )(*flat)


def after(values, *deps):
    return lax.optimization_barrier((values, deps))[0]


def on_device(tokens, picks, counts, score, w_in, w_out, cotan):
    routed = picks.shape[0]
    n_tok = tokens.shape[0]

    own_mine, me = take_rows(tokens, picks, counts, score, cotan)
    w_in, w_out = hold(*after((w_in, w_out), own_mine))
    near_mine = move_lane(own_mine, 1)
    own_other = swap_core(own_mine)
    own = hidden_units([[own_mine], [own_other]], w_in, w_out)

    near_other = move_lane(own_other, 1)
    near_mine = after(near_mine, own)
    far_mine = move_lane(near_mine, 1)
    swapped_mine = [swap_core(near_mine[:1]), swap_core(near_mine[1:])]
    own_terms = row_terms(own[0], own[1], w_in, w_out, routed, 1)
    own_got = swap_core(own_terms[1])
    near_mine, swapped_mine = after((near_mine, swapped_mine), own_terms)
    near = hidden_units([[near_mine], swapped_mine], w_in, w_out)
    near_terms = row_terms(near[0], near[1], w_in, w_out, routed, 3)

    near_other = after(near_other, near)
    swapped_other = [swap_core(near_other[:1]), swap_core(near_other[1:])]
    swapped_other, own_got = after((swapped_other, own_got), near_terms)
    other = hidden_units([[near_other], swapped_other], w_in, w_out)
    near_terms = row_terms(other[0], other[1], w_in, w_out, routed, 3, 1, near_terms)

    far_mine = after(far_mine, other)
    far_packs = after([far_mine, swap_core(far_mine)], near_terms)
    far = hidden_units([[p] for p in far_packs], w_in, w_out)
    last_terms = row_terms(far[0], far[1], w_in, w_out, routed, 3, 2, near_terms)
    last_got = swap_core(last_terms[1])

    all_packs = [own_mine, own_other, near_mine, swapped_mine[0], near_other, swapped_other[0]] + far_packs
    hidden, dpre, turned = ([u[i] for u in (own, near, other, far)] for i in range(3))
    all_packs, dpre = after((all_packs, dpre), last_terms)
    in_up, in_down = in_blocks(me, all_packs, dpre, FIRST_STEP)
    in_below, in_above = move_x(in_up, 1), move_x(in_down, -1)

    hidden, turned = after((hidden, turned), in_up, in_down)
    out_up, out_down = out_blocks(me, hidden, turned, FIRST_STEP)
    out_below, out_above = move_y(out_up, 1), move_y(out_down, -1)

    last_got = after(last_got, out_up, out_down)
    to_far = (last_terms[0][2].astype(F32) + last_got[2].astype(F32)).astype(BF16)
    z_far = move_lane(to_far, -1)
    all_packs, dpre = after((all_packs, dpre), to_far)
    in_later = in_blocks(me, all_packs, dpre, LATER_STEP)[0]
    z_far = after(z_far, in_later)
    passed = jnp.pad(z_far.astype(F32)[None], ((0, 1), (0, 0), (0, 0), (0, 0)))
    to_near = (last_terms[0][:2].astype(F32) + last_got[:2].astype(F32) + passed).astype(BF16)
    z_near = move_lane(to_near, -1)
    hidden, turned = after((hidden, turned), to_near)
    out_later = out_blocks(me, hidden, turned, LATER_STEP)[0]

    def second_hop(later, from_below, from_above, move):
        up = (later[0].astype(F32) + from_below[0].astype(F32)).astype(BF16)
        down = (later[1].astype(F32) + from_above[0].astype(F32)).astype(BF16)
        return move(up, 1), move(down, -1), up, down

    in_below, in_above, out_below, out_above = after((in_below, in_above, out_below, out_above), out_later)
    in_hops = second_hop(in_later, in_below, in_above, move_x)
    out_hops = second_hop(out_later, out_below, out_above, move_y)
    in_total = ring_total(me, in_later, in_hops[0], in_above, in_below, in_hops[1], True)
    out_hops = after(out_hops[:2], in_total)
    z_near = after(z_near, in_total, out_hops)
    z_other = swap_core(z_near[1])

    def second_stage(total, move):
        keep, following, previous, far = total
        return keep, move(far, 2), move(following, 1), move(previous, -1)

    out_total = ring_total(me, out_later, out_hops[0], out_above, out_below, out_hops[1], False)
    in_total, out_total = after((in_total, out_total), z_other)
    in_parts = second_stage(in_total, move_y)
    out_parts = second_stage(out_total, move_x)

    back = (
        own_terms[0][0].astype(F32) + own_got[0].astype(F32) + z_near[0].astype(F32) + z_other.astype(F32)
    ).astype(BF16)
    ffn = back[0].astype(F32)
    heavy = (score[:, None] * ffn).astype(BF16)
    grad_score = jnp.sum(cotan.astype(F32) * ffn, axis=1)
    place = picks[:, None] == jnp.arange(n_tok, dtype=jnp.int32)[None, :]
    grad_x = dot(place.astype(BF16), back[1], ((0,), (0,))).astype(BF16)
    in_parts, out_parts = after((in_parts, out_parts), heavy, grad_x)
    grad_in, grad_out = add_up(in_parts, out_parts)
    return (heavy, grad_x, grad_score, grad_in, grad_out)


def solution(mesh):
    placed = (
        P(("ctx", "head"), None),
        P(("ctx", "head")),
        P(("ctx", "head")),
        P(("ctx", "head")),
        P(None, "head"),
        P("head", None),
        P(("ctx", "head"), None),
    )
    return jax.shard_map(
        on_device,
        mesh=mesh,
        in_specs=placed,
        out_specs=(
            P(("ctx", "head"), None),
            P(("ctx", "head"), None),
            P(("ctx", "head")),
            P("ctx", "head"),
            P("head", "ctx"),
        ),
        check_vma=False,
    )
```

```python
import functools

import jax
import jax.numpy as jnp
from jax import lax
from jax.experimental import pallas as pl
from jax.experimental.pallas import tpu as pltpu
from jax.sharding import PartitionSpec as P

F32 = jnp.float32
BF16 = jnp.bfloat16
SIDE = 4
MIB = 1024 * 1024
LITTLE = pl.CostEstimate(flops=1, bytes_accessed=1, transcendentals=0)


def gelu_parts(u):
    c = 0.7978845608
    t = jnp.tanh(c * (u + 0.044715 * u * u * u))
    value = 0.5 * u * (1.0 + t)
    slope = 0.5 * (1.0 + t) + 0.5 * u * (1.0 - t * t) * c * (1.0 + 3.0 * 0.044715 * u * u)
    return (value, slope)


def move_x(v, by):
    perm = [(x * SIDE + y, ((x + by) % SIDE) * SIDE + y) for x in range(SIDE) for y in range(SIDE)]
    return lax.ppermute(v, "ctx", perm)


def move_y(v, by):
    perm = [(x * SIDE + y, x * SIDE + (y + by) % SIDE) for x in range(SIDE) for y in range(SIDE)]
    return lax.ppermute(v, "ctx", perm)


def move_lane(v, by):
    perm = [(z * 2 + c, ((z + (by if c == 0 else -by)) % SIDE) * 2 + c) for z in range(SIDE) for c in range(2)]
    return lax.ppermute(v, "head", perm)


def swap_core(v):
    return lax.ppermute(v, "head", [(i, i ^ 1) for i in range(2 * SIDE)])


def dot(a, b, dims):
    return lax.dot_general(a, b, ((dims[0], dims[1]), ((), ())), preferred_element_type=F32)


def params(mib):
    return pltpu.CompilerParams(vmem_limit_bytes=mib * MIB)


def whole(a):
    return pl.BlockSpec(a.shape, lambda *_: (0,) * a.ndim)


def take_rows(tokens, picks, counts, score, cotan):
    routed = picks.shape[0]
    n_tok, width = tokens.shape

    def body(counts_ref, tokens_ref, picks_ref, score_ref, cotan_ref, out_ref, me_ref):
        me_ref[0] = lax.axis_index("ctx").astype(jnp.int32)
        me_ref[1] = lax.axis_index("head").astype(jnp.int32)
        places = lax.broadcasted_iota(jnp.int32, (n_tok, routed), 0)
        slots = lax.broadcasted_iota(jnp.int32, (n_tok, routed), 1)
        hit = (places == picks_ref[...]) & (slots < counts_ref[0])
        one_hot = jnp.where(hit, 1.0, 0.0).astype(BF16)
        out_ref[0] = dot(one_hot, tokens_ref[...], ((0,), (0,))).astype(BF16)
        across = lax.broadcasted_iota(jnp.int32, (routed, routed), 0)
        along = lax.broadcasted_iota(jnp.int32, (routed, routed), 1)
        kept = (across == along) & (along < counts_ref[0])
        factor = jnp.sum(jnp.where(kept, score_ref[...], 0.0), axis=1, keepdims=True)
        out_ref[1] = (factor * cotan_ref[...].astype(F32)).astype(BF16)

    return pl.pallas_call(
        body,
        grid_spec=pltpu.PrefetchScalarGridSpec(
            num_scalar_prefetch=1,
            grid=(1,),
            in_specs=[
                whole(tokens),
                pl.BlockSpec((1, routed), lambda i, c: (0, 0)),
                pl.BlockSpec((1, routed), lambda i, c: (0, 0)),
                whole(cotan),
            ],
            out_specs=[
                pl.BlockSpec((2, routed, width), lambda i, c: (0, 0, 0)),
                pl.BlockSpec(memory_space=pltpu.SMEM),
            ],
        ),
        out_shape=[jax.ShapeDtypeStruct((2, routed, width), BF16), jax.ShapeDtypeStruct((2,), jnp.int32)],
        compiler_params=params(60),
        cost_estimate=LITTLE,
        name="take_rows",
    )(counts, tokens, picks[None, :], score[None, :], cotan)


IN_VMEM = pl.BlockSpec(memory_space=pltpu.VMEM)
IN_SMEM = pl.BlockSpec(memory_space=pltpu.SMEM)


def held(a):
    return pltpu.with_memory_space_constraint(a, pltpu.VMEM)


def on_held(body, arrays, shapes, name, me=None, spare=(), aliases={}):
    first = [] if me is None else [me]
    return pl.pallas_call(
        body,
        in_specs=[IN_SMEM] * len(first) + [IN_VMEM] * len(arrays) + [pl.BlockSpec(memory_space=pl.ANY)] * len(spare),
        out_specs=[IN_VMEM] * len(shapes),
        out_shape=[pltpu.VMEM(shape, dtype) for shape, dtype in shapes],
        input_output_aliases=aliases,
        compiler_params=params(12),
        cost_estimate=LITTLE,
        name=name,
    )(*first, *[held(a) for a in arrays], *[held(a) for a in spare])


def repeat(count, step, unrolled):
    if unrolled:
        for i in range(count):
            step(i)
    else:
        lax.fori_loop(0, count, lambda i, c: (step(i), c)[1], 0)


def span(i, size):
    at = i * size
    return pl.ds(at if isinstance(i, int) else pl.multiple_of(at, size), size)


def hidden_units(packs, w_in, w_out, unrolled=False):
    halves = [(i, h) for i, p in enumerate(packs) for h in range(len(p))]
    at = {p: k for k, p in enumerate(halves)}
    where_r = [at[(i, 0)] for i in range(len(packs))]
    where_d = [at[(i, len(p) - 1)] for i, p in enumerate(packs)]
    flat = [a for p in packs for a in p]
    n = len(packs)
    _, piece, width = flat[0].shape
    count = n * piece
    hid = w_in.shape[1]
    tile = hid // SIDE
    quarter = width // SIDE
    strip = quarter // SIDE

    def body(*refs):
        last = [refs[k].shape[0] - 1 for k in where_d]
        r = jnp.concatenate([refs[k][0] for k in where_r], axis=0)
        d = jnp.concatenate([refs[k][i] for k, i in zip(where_d, last)], axis=0)
        win_ref, wout_ref, hidden_ref, dpre_ref, turned_ref = refs[len(flat) :]

        def step(j):
            cols = span(j, tile)
            pre = dot(r, win_ref[:, cols], ((1,), (0,)))
            dhid = dot(d, wout_ref[cols, :], ((1,), (1,)))
            value, slope = gelu_parts(pre)
            hidden_ref[:, cols] = value.astype(BF16)
            dpre_ref[:, cols] = (dhid * slope).astype(BF16)
            for x in range(SIDE):
                to = span(j * SIDE + x, strip)
                for k in range(n):
                    turned_ref[pl.ds(k * piece, piece), to] = refs[where_d[k]][last[k], :, span(x * SIDE + j, strip)]

        repeat(SIDE, step, unrolled)

    shapes = [((count, hid), BF16), ((count, hid), BF16), ((count, width), BF16)]
    return on_held(body, flat + [w_in, w_out], shapes, "hidden_units")


def hold(w_in, w_out):
    def body(win_ref, wout_ref, win_out, wout_out, sems):
        copies = [
            pltpu.make_async_copy(win_ref, win_out, sems.at[0]),
            pltpu.make_async_copy(wout_ref, wout_out, sems.at[1]),
        ]
        for copy in copies:
            copy.start()
        for copy in copies:
            copy.wait()

    return pl.pallas_call(
        body,
        in_specs=[pl.BlockSpec(memory_space=pl.ANY)] * 2,
        out_specs=[pl.BlockSpec(memory_space=pltpu.VMEM)] * 2,
        out_shape=[pltpu.VMEM(w.shape, w.dtype) for w in (w_in, w_out)],
        scratch_shapes=[pltpu.SemaphoreType.DMA((2,))],
        compiler_params=params(4),
        cost_estimate=LITTLE,
        name="hold_weights",
    )(pltpu.with_memory_space_constraint(w_in, pltpu.HBM), pltpu.with_memory_space_constraint(w_out, pltpu.HBM))


def row_terms(hidden, dpre, w_in, w_out, piece, groups, first=0, held_terms=(), unrolled=False):
    count, hid = hidden.shape
    width = w_in.shape[0]
    n = count // (2 * piece)
    tile = width // SIDE

    def body(hidden_ref, dpre_ref, win_ref, wout_ref, *refs):
        outs = refs[len(held_terms) :]

        def step(j):
            cols = span(j, tile)
            ffn = dot(hidden_ref[...], wout_ref[:, cols], ((1,), (0,))).astype(BF16)
            dx = dot(dpre_ref[...], win_ref[cols, :], ((1,), (1,))).astype(BF16)
            for h in range(2):
                for k in range(n):
                    for s, v in enumerate((ffn, dx)):
                        outs[h][first + k, s, :, cols] = v[(h * n + k) * piece : (h * n + k + 1) * piece]

        repeat(SIDE, step, unrolled)

    shapes = [((groups, 2, piece, width), BF16)] * 2
    aliases = {4 + i: i for i in range(len(held_terms))}
    return on_held(body, [hidden, dpre, w_in, w_out], shapes, "row_terms", spare=held_terms, aliases=aliases)


FIRST_STEP = ((2, 0), (2, 1), (1, 1), (3, 0))
LATER_STEP = ((1, 0), (3, 1), (0, 0), (0, 1))


def make_blocks(steps, outs, make):
    if steps is FIRST_STEP:
        for i, (place, half) in enumerate(steps):
            outs[i % 2][i // 2] = make(place, half).astype(BF16)
    else:

        def step(i):
            place = jnp.where(i >= 2, 0, jnp.where(i == 0, 1, 3))
            half = jnp.where((i == 1) | (i == 3), 1, 0)
            outs[0][i] = make(place, half).astype(BF16)

        repeat(len(steps), step, False)


def block_shapes(steps, block):
    return [((2,) + block, BF16)] * 2 if steps is FIRST_STEP else [((len(steps),) + block, BF16)]


def in_blocks(me, packs, dpre, steps):
    n = len(packs)
    _, piece, width = packs[0].shape
    hid = dpre[0].shape[1]
    size = width // (2 * SIDE)
    each = n // len(dpre)

    def body(me_ref, *refs):
        def make(place, half):
            to = 2 * lax.rem(me_ref[0] // SIDE + place, SIDE) + half
            cols = pl.ds(pl.multiple_of(to * size, size), size)
            term = None
            for c in range(len(dpre)):
                r = jnp.concatenate([ref[0, :, cols] for ref in refs[c * each : (c + 1) * each]], axis=0)
                part = dot(r, refs[n + c][...], ((0,), (0,)))
                term = part if term is None else term + part
            return term

        make_blocks(steps, refs[n + len(dpre) :], make)

    return on_held(body, packs + dpre, block_shapes(steps, (size, hid)), "in_blocks", me)


def out_blocks(me, hidden, turned, steps):
    n = len(hidden)
    hid = hidden[0].shape[1]
    quarter = turned[0].shape[1] // SIDE

    def body(me_ref, *refs):
        def make(place, half):
            to = lax.rem(lax.rem(me_ref[0], SIDE) + place, SIDE)
            cols = pl.ds(pl.multiple_of(to * quarter, quarter), quarter)
            term = None
            for c in range(n):
                part = dot(refs[c][:, span(half, hid // 2)], refs[n + c][:, cols], ((0,), (0,)))
                term = part if term is None else term + part
            return term

        make_blocks(steps, refs[2 * n :], make)

    return on_held(body, hidden + turned, block_shapes(steps, (hid // 2, quarter)), "out_blocks", me)


def ring_total(me, later, below0, above0, below1, above1, rowwise):
    block = later.shape[1:]
    if rowwise:
        cut = (2 * block[0] // SIDE, block[1])
    else:
        cut = (2 * block[0], block[1] // SIDE)

    def body(me_ref, later_ref, b0, a0, b1, a1, keep_ref, next_ref, prev_ref, far_ref, sum_ref):
        half = block[0]
        rows = half // SIDE

        def step(j):
            cut_j = span(j, rows)
            first = later_ref[2, cut_j].astype(F32) + b0[cut_j].astype(F32) + a0[1, cut_j].astype(F32)
            second = later_ref[3, cut_j].astype(F32) + b1[1, cut_j].astype(F32) + a1[cut_j].astype(F32)
            sum_ref[cut_j, :] = first
            sum_ref[span(j + SIDE, rows), :] = second

        repeat(SIDE, step, False)
        if rowwise:
            at = lax.rem(me_ref[0], SIDE)
        else:
            at = me_ref[0] // SIDE
        for k, ref in ((0, keep_ref), (1, next_ref), (3, prev_ref), (2, far_ref)):
            to = lax.rem(at + k, SIDE)
            if rowwise:
                v = sum_ref[pl.ds(pl.multiple_of(to * cut[0], cut[0]), cut[0]), :]
            else:
                v = sum_ref[:, pl.ds(pl.multiple_of(to * cut[1], cut[1]), cut[1])]
            ref[...] = v.astype(ref.dtype)

    return pl.pallas_call(
        body,
        in_specs=[IN_SMEM] + [IN_VMEM] * 5,
        out_specs=[IN_VMEM] * 4,
        out_shape=[pltpu.VMEM(cut, F32)] + [pltpu.VMEM(cut, BF16)] * 3,
        scratch_shapes=[pltpu.VMEM((2 * block[0], block[1]), F32)],
        compiler_params=params(12),
        cost_estimate=LITTLE,
        name="ring_total",
    )(me, *[held(a) for a in (later, below0, above0, below1, above1)])


def add_up(*groups):
    flat = [a for g in groups for a in g]

    def body(*refs):
        at = 0
        for g, out_ref in zip(groups, refs[len(flat) :]):
            total = refs[at][...].astype(F32)
            for ref in refs[at + 1 : at + len(g)]:
                total += ref[...].astype(F32)
            out_ref[...] = total
            at += len(g)

    return pl.pallas_call(
        body,
        grid=(1,),
        in_specs=[whole(a) for a in flat],
        out_specs=[whole(g[0]) for g in groups],
        out_shape=[jax.ShapeDtypeStruct(g[0].shape, F32) for g in groups],
        compiler_params=params(10),
        cost_estimate=LITTLE,
        name="add_up",
    )(*flat)


def after(values, *deps):
    return lax.optimization_barrier((values, deps))[0]


def on_device(tokens, picks, counts, score, w_in, w_out, cotan):
    routed = picks.shape[0]
    n_tok = tokens.shape[0]

    own_mine, me = take_rows(tokens, picks, counts, score, cotan)
    w_in, w_out = hold(*after((w_in, w_out), own_mine))
    near_mine = move_lane(own_mine, 1)
    own_other = swap_core(own_mine)
    own = hidden_units([[own_mine], [own_other]], w_in, w_out)

    near_other = move_lane(own_other, 1)
    near_mine = after(near_mine, own)
    far_mine = move_lane(near_mine, 1)
    swapped_mine = [swap_core(near_mine[:1]), swap_core(near_mine[1:])]
    own_terms = row_terms(own[0], own[1], w_in, w_out, routed, 1)
    own_got = swap_core(own_terms[1])
    near_mine, swapped_mine = after((near_mine, swapped_mine), own_terms)
    near = hidden_units([[near_mine], swapped_mine], w_in, w_out)
    near_terms = row_terms(near[0], near[1], w_in, w_out, routed, 3)

    near_other = after(near_other, near)
    swapped_other = [swap_core(near_other[:1]), swap_core(near_other[1:])]
    swapped_other, own_got = after((swapped_other, own_got), near_terms)
    other = hidden_units([[near_other], swapped_other], w_in, w_out)
    near_terms = row_terms(other[0], other[1], w_in, w_out, routed, 3, 1, near_terms)

    far_mine = after(far_mine, other)
    far_packs = after([far_mine, swap_core(far_mine)], near_terms)
    far = hidden_units([[p] for p in far_packs], w_in, w_out, True)
    last_terms = row_terms(far[0], far[1], w_in, w_out, routed, 3, 2, near_terms, True)
    last_got = swap_core(last_terms[1])

    all_packs = [own_mine, own_other, near_mine, swapped_mine[0], near_other, swapped_other[0]] + far_packs
    hidden, dpre, turned = ([u[i] for u in (own, near, other, far)] for i in range(3))
    all_packs, dpre = after((all_packs, dpre), last_terms)
    in_up, in_down = in_blocks(me, all_packs, dpre, FIRST_STEP)
    in_below, in_above = move_x(in_up, 1), move_x(in_down, -1)

    hidden, turned = after((hidden, turned), in_up, in_down)
    out_up, out_down = out_blocks(me, hidden, turned, FIRST_STEP)
    out_below, out_above = move_y(out_up, 1), move_y(out_down, -1)

    last_got = after(last_got, out_up, out_down)
    to_far = (last_terms[0][2].astype(F32) + last_got[2].astype(F32)).astype(BF16)
    z_far = move_lane(to_far, -1)
    all_packs, dpre = after((all_packs, dpre), to_far)
    in_later = in_blocks(me, all_packs, dpre, LATER_STEP)[0]
    z_far = after(z_far, in_later)
    passed = jnp.pad(z_far.astype(F32)[None], ((0, 1), (0, 0), (0, 0), (0, 0)))
    to_near = (last_terms[0][:2].astype(F32) + last_got[:2].astype(F32) + passed).astype(BF16)
    z_near = move_lane(to_near, -1)
    hidden, turned = after((hidden, turned), to_near)
    out_later = out_blocks(me, hidden, turned, LATER_STEP)[0]

    def second_hop(later, from_below, from_above, move):
        up = (later[0].astype(F32) + from_below[0].astype(F32)).astype(BF16)
        down = (later[1].astype(F32) + from_above[0].astype(F32)).astype(BF16)
        return move(up, 1), move(down, -1), up, down

    in_below, in_above, out_below, out_above = after((in_below, in_above, out_below, out_above), out_later)
    in_hops = second_hop(in_later, in_below, in_above, move_x)
    out_hops = second_hop(out_later, out_below, out_above, move_y)
    in_total = ring_total(me, in_later, in_hops[0], in_above, in_below, in_hops[1], True)
    out_hops = after(out_hops[:2], in_total)
    z_near = after(z_near, in_total, out_hops)
    z_other = swap_core(z_near[1])

    def second_stage(total, move):
        keep, following, previous, far = total
        return keep, move(far, 2), move(following, 1), move(previous, -1)

    out_total = ring_total(me, out_later, out_hops[0], out_above, out_below, out_hops[1], False)
    in_total, out_total = after((in_total, out_total), z_other)
    in_parts = second_stage(in_total, move_y)
    out_parts = second_stage(out_total, move_x)

    back = (
        own_terms[0][0].astype(F32) + own_got[0].astype(F32) + z_near[0].astype(F32) + z_other.astype(F32)
    ).astype(BF16)
    ffn = back[0].astype(F32)
    heavy = (score[:, None] * ffn).astype(BF16)
    grad_score = jnp.sum(cotan.astype(F32) * ffn, axis=1)
    place = picks[:, None] == jnp.arange(n_tok, dtype=jnp.int32)[None, :]
    grad_x = dot(place.astype(BF16), back[1], ((0,), (0,))).astype(BF16)
    in_parts, out_parts = after((in_parts, out_parts), heavy, grad_x)
    grad_in, grad_out = add_up(in_parts, out_parts)
    return (heavy, grad_x, grad_score, grad_in, grad_out)


def solution(mesh):
    placed = (
        P(("ctx", "head"), None),
        P(("ctx", "head")),
        P(("ctx", "head")),
        P(("ctx", "head")),
        P(None, "head"),
        P("head", None),
        P(("ctx", "head"), None),
    )
    return jax.shard_map(
        on_device,
        mesh=mesh,
        in_specs=placed,
        out_specs=(
            P(("ctx", "head"), None),
            P(("ctx", "head"), None),
            P(("ctx", "head")),
            P("ctx", "head"),
            P("head", "ctx"),
        ),
        check_vma=False,
    )
```

```python
import functools

import jax
import jax.numpy as jnp
from jax import lax
from jax.experimental import pallas as pl
from jax.experimental.pallas import tpu as pltpu
from jax.sharding import PartitionSpec as P

F32 = jnp.float32
BF16 = jnp.bfloat16
SIDE = 4
MIB = 1024 * 1024
LITTLE = pl.CostEstimate(flops=1, bytes_accessed=1, transcendentals=0)
IN_VMEM = pl.BlockSpec(memory_space=pltpu.VMEM)
IN_SMEM = pl.BlockSpec(memory_space=pltpu.SMEM)


def gelu_parts(u):
    c = 0.7978845608
    t = jnp.tanh(c * (u + 0.044715 * u * u * u))
    value = 0.5 * u * (1.0 + t)
    slope = 0.5 * (1.0 + t) + 0.5 * u * (1.0 - t * t) * c * (1.0 + 3.0 * 0.044715 * u * u)
    return (value, slope)


def move_x(v, by):
    perm = [(x * SIDE + y, ((x + by) % SIDE) * SIDE + y) for x in range(SIDE) for y in range(SIDE)]
    return lax.ppermute(v, "ctx", perm)


def move_y(v, by):
    perm = [(x * SIDE + y, x * SIDE + (y + by) % SIDE) for x in range(SIDE) for y in range(SIDE)]
    return lax.ppermute(v, "ctx", perm)


def move_lane(v, by):
    perm = [(z * 2 + c, ((z + (by if c == 0 else -by)) % SIDE) * 2 + c) for z in range(SIDE) for c in range(2)]
    return lax.ppermute(v, "head", perm)


def swap_core(v):
    return lax.ppermute(v, "head", [(i, i ^ 1) for i in range(2 * SIDE)])


def dot(a, b, dims):
    return lax.dot_general(a, b, ((dims[0], dims[1]), ((), ())), preferred_element_type=F32)


def params(mib):
    return pltpu.CompilerParams(vmem_limit_bytes=mib * MIB)


def whole(a):
    return pl.BlockSpec(a.shape, lambda *_: (0,) * a.ndim)


def take_rows(tokens, picks, counts, score, cotan):
    routed = picks.shape[0]
    n_tok, width = tokens.shape
    parts = 2
    part = width // parts

    def body(counts_ref, picks_hbm, score_hbm, tokens_ref, cotan_ref, out_ref, me_ref, *scratch):
        rows_in, cotan_in, picks_ref, score_ref, sems = scratch
        small = [
            pltpu.make_async_copy(picks_hbm, picks_ref, sems.at[parts + 1]),
            pltpu.make_async_copy(score_hbm, score_ref, sems.at[parts + 2]),
        ]
        for copy in small:
            copy.start()
        copies = [pltpu.make_async_copy(cotan_ref, cotan_in, sems.at[parts])]
        for p in range(parts):
            cols = pl.ds(p * part, part)
            copies.append(pltpu.make_async_copy(tokens_ref.at[:, cols], rows_in.at[p], sems.at[p]))
        for copy in copies:
            copy.start()
        me_ref[0] = lax.axis_index("ctx").astype(jnp.int32)
        me_ref[1] = lax.axis_index("head").astype(jnp.int32)
        for copy in small:
            copy.wait()
        places = lax.broadcasted_iota(jnp.int32, (n_tok, routed), 0)
        slots = lax.broadcasted_iota(jnp.int32, (n_tok, routed), 1)
        hit = (places == picks_ref[...]) & (slots < counts_ref[0])
        one_hot = jnp.where(hit, 1.0, 0.0).astype(BF16)
        across = lax.broadcasted_iota(jnp.int32, (routed, routed), 0)
        along = lax.broadcasted_iota(jnp.int32, (routed, routed), 1)
        kept = (across == along) & (along < counts_ref[0])
        factor = jnp.sum(jnp.where(kept, score_ref[...], 0.0), axis=1, keepdims=True)
        copies[0].wait()
        out_ref[1] = (factor * cotan_in[...].astype(F32)).astype(BF16)
        for p in range(parts):
            copies[1 + p].wait()
            out_ref[0, :, pl.ds(p * part, part)] = dot(one_hot, rows_in[p], ((0,), (0,))).astype(BF16)

    in_hbm = pl.BlockSpec(memory_space=pl.ANY)
    return pl.pallas_call(
        body,
        in_specs=[IN_SMEM] + [in_hbm] * 4,
        out_specs=[IN_VMEM, IN_SMEM],
        out_shape=[pltpu.VMEM((2, routed, width), BF16), jax.ShapeDtypeStruct((2,), jnp.int32)],
        scratch_shapes=[
            pltpu.VMEM((parts, n_tok, part), BF16),
            pltpu.VMEM((routed, width), BF16),
            pltpu.VMEM((1, routed), jnp.int32),
            pltpu.VMEM((1, routed), F32),
            pltpu.SemaphoreType.DMA((parts + 3,)),
        ],
        compiler_params=params(12),
        cost_estimate=LITTLE,
        name="take_rows",
    )(
        counts,
        *[pltpu.with_memory_space_constraint(a, pltpu.HBM) for a in (picks[None, :], score[None, :], tokens, cotan)],
    )


def held(a):
    return pltpu.with_memory_space_constraint(a, pltpu.VMEM)


def on_held(body, arrays, shapes, name, me=None, spare=(), aliases={}):
    first = [] if me is None else [me]
    return pl.pallas_call(
        body,
        in_specs=[IN_SMEM] * len(first) + [IN_VMEM] * len(arrays) + [pl.BlockSpec(memory_space=pl.ANY)] * len(spare),
        out_specs=[IN_VMEM] * len(shapes),
        out_shape=[pltpu.VMEM(shape, dtype) for shape, dtype in shapes],
        input_output_aliases=aliases,
        compiler_params=params(12),
        cost_estimate=LITTLE,
        name=name,
    )(*first, *[held(a) for a in arrays], *[held(a) for a in spare])


def repeat(count, step, unrolled):
    if unrolled:
        for i in range(count):
            step(i)
    else:
        lax.fori_loop(0, count, lambda i, c: (step(i), c)[1], 0)


def span(i, size):
    at = i * size
    return pl.ds(at if isinstance(i, int) else pl.multiple_of(at, size), size)


def hidden_units(packs, w_in, w_out, unrolled=False):
    halves = [(i, h) for i, p in enumerate(packs) for h in range(len(p))]
    at = {p: k for k, p in enumerate(halves)}
    where_r = [at[(i, 0)] for i in range(len(packs))]
    where_d = [at[(i, len(p) - 1)] for i, p in enumerate(packs)]
    flat = [a for p in packs for a in p]
    n = len(packs)
    _, piece, width = flat[0].shape
    count = n * piece
    hid = w_in.shape[1]
    tile = hid // SIDE
    quarter = width // SIDE
    strip = quarter // SIDE

    def body(*refs):
        last = [refs[k].shape[0] - 1 for k in where_d]
        r = jnp.concatenate([refs[k][0] for k in where_r], axis=0)
        d = jnp.concatenate([refs[k][i] for k, i in zip(where_d, last)], axis=0)
        win_ref, wout_ref, hidden_ref, dpre_ref, turned_ref = refs[len(flat) :]

        def step(j):
            cols = span(j, tile)
            pre = dot(r, win_ref[:, cols], ((1,), (0,)))
            dhid = dot(d, wout_ref[cols, :], ((1,), (1,)))
            value, slope = gelu_parts(pre)
            hidden_ref[:, cols] = value.astype(BF16)
            dpre_ref[:, cols] = (dhid * slope).astype(BF16)
            for x in range(SIDE):
                to = span(j * SIDE + x, strip)
                for k in range(n):
                    turned_ref[pl.ds(k * piece, piece), to] = refs[where_d[k]][last[k], :, span(x * SIDE + j, strip)]

        repeat(SIDE, step, unrolled)

    shapes = [((count, hid), BF16), ((count, hid), BF16), ((count, width), BF16)]
    return on_held(body, flat + [w_in, w_out], shapes, "hidden_units")


def hold(w_in, w_out):
    def body(win_ref, wout_ref, win_out, wout_out, sems):
        copies = [
            pltpu.make_async_copy(win_ref, win_out, sems.at[0]),
            pltpu.make_async_copy(wout_ref, wout_out, sems.at[1]),
        ]
        for copy in copies:
            copy.start()
        for copy in copies:
            copy.wait()

    return pl.pallas_call(
        body,
        in_specs=[pl.BlockSpec(memory_space=pl.ANY)] * 2,
        out_specs=[pl.BlockSpec(memory_space=pltpu.VMEM)] * 2,
        out_shape=[pltpu.VMEM(w.shape, w.dtype) for w in (w_in, w_out)],
        scratch_shapes=[pltpu.SemaphoreType.DMA((2,))],
        compiler_params=params(4),
        cost_estimate=LITTLE,
        name="hold_weights",
    )(pltpu.with_memory_space_constraint(w_in, pltpu.HBM), pltpu.with_memory_space_constraint(w_out, pltpu.HBM))


def row_terms(hidden, dpre, w_in, w_out, piece, groups, first=0, held_terms=(), unrolled=False):
    count, hid = hidden.shape
    width = w_in.shape[0]
    n = count // (2 * piece)
    tile = width // SIDE

    def body(hidden_ref, dpre_ref, win_ref, wout_ref, *refs):
        outs = refs[len(held_terms) :]

        def step(j):
            cols = span(j, tile)
            ffn = dot(hidden_ref[...], wout_ref[:, cols], ((1,), (0,))).astype(BF16)
            dx = dot(dpre_ref[...], win_ref[cols, :], ((1,), (1,))).astype(BF16)
            for h in range(2):
                for k in range(n):
                    for s, v in enumerate((ffn, dx)):
                        outs[h][first + k, s, :, cols] = v[(h * n + k) * piece : (h * n + k + 1) * piece]

        repeat(SIDE, step, unrolled)

    shapes = [((groups, 2, piece, width), BF16)] * 2
    aliases = {4 + i: i for i in range(len(held_terms))}
    return on_held(body, [hidden, dpre, w_in, w_out], shapes, "row_terms", spare=held_terms, aliases=aliases)


FIRST_STEP = ((2, 0), (2, 1), (1, 1), (3, 0))
LATER_STEP = ((1, 0), (3, 1), (0, 0), (0, 1))


def make_blocks(steps, outs, make):
    if steps is FIRST_STEP:
        for i, (place, half) in enumerate(steps):
            outs[i % 2][i // 2] = make(place, half).astype(BF16)
    else:

        def step(i):
            place = jnp.where(i >= 2, 0, jnp.where(i == 0, 1, 3))
            half = jnp.where((i == 1) | (i == 3), 1, 0)
            outs[0][i] = make(place, half).astype(BF16)

        repeat(len(steps), step, False)


def block_shapes(steps, block):
    return [((2,) + block, BF16)] * 2 if steps is FIRST_STEP else [((len(steps),) + block, BF16)]


def in_blocks(me, packs, dpre, steps):
    n = len(packs)
    _, piece, width = packs[0].shape
    hid = dpre[0].shape[1]
    size = width // (2 * SIDE)
    each = n // len(dpre)

    def body(me_ref, *refs):
        def make(place, half):
            to = 2 * lax.rem(me_ref[0] // SIDE + place, SIDE) + half
            cols = pl.ds(pl.multiple_of(to * size, size), size)
            term = None
            for c in range(len(dpre)):
                r = jnp.concatenate([ref[0, :, cols] for ref in refs[c * each : (c + 1) * each]], axis=0)
                part = dot(r, refs[n + c][...], ((0,), (0,)))
                term = part if term is None else term + part
            return term

        make_blocks(steps, refs[n + len(dpre) :], make)

    return on_held(body, packs + dpre, block_shapes(steps, (size, hid)), "in_blocks", me)


def out_blocks(me, hidden, turned, steps):
    n = len(hidden)
    hid = hidden[0].shape[1]
    quarter = turned[0].shape[1] // SIDE

    def body(me_ref, *refs):
        def make(place, half):
            to = lax.rem(lax.rem(me_ref[0], SIDE) + place, SIDE)
            cols = pl.ds(pl.multiple_of(to * quarter, quarter), quarter)
            term = None
            for c in range(n):
                part = dot(refs[c][:, span(half, hid // 2)], refs[n + c][:, cols], ((0,), (0,)))
                term = part if term is None else term + part
            return term

        make_blocks(steps, refs[2 * n :], make)

    return on_held(body, hidden + turned, block_shapes(steps, (hid // 2, quarter)), "out_blocks", me)


def ring_total(me, later, below0, above0, below1, above1, rowwise):
    block = later.shape[1:]
    if rowwise:
        cut = (2 * block[0] // SIDE, block[1])
    else:
        cut = (2 * block[0], block[1] // SIDE)

    def body(me_ref, later_ref, b0, a0, b1, a1, keep_ref, next_ref, prev_ref, far_ref, sum_ref):
        half = block[0]
        rows = half // SIDE

        def step(j):
            cut_j = span(j, rows)
            first = later_ref[2, cut_j].astype(F32) + b0[cut_j].astype(F32) + a0[1, cut_j].astype(F32)
            second = later_ref[3, cut_j].astype(F32) + b1[1, cut_j].astype(F32) + a1[cut_j].astype(F32)
            sum_ref[cut_j, :] = first
            sum_ref[span(j + SIDE, rows), :] = second

        repeat(SIDE, step, False)
        if rowwise:
            at = lax.rem(me_ref[0], SIDE)
        else:
            at = me_ref[0] // SIDE
        for k, ref in ((0, keep_ref), (1, next_ref), (3, prev_ref), (2, far_ref)):
            to = lax.rem(at + k, SIDE)
            if rowwise:
                v = sum_ref[pl.ds(pl.multiple_of(to * cut[0], cut[0]), cut[0]), :]
            else:
                v = sum_ref[:, pl.ds(pl.multiple_of(to * cut[1], cut[1]), cut[1])]
            ref[...] = v.astype(ref.dtype)

    return pl.pallas_call(
        body,
        in_specs=[IN_SMEM] + [IN_VMEM] * 5,
        out_specs=[IN_VMEM] * 4,
        out_shape=[pltpu.VMEM(cut, F32)] + [pltpu.VMEM(cut, BF16)] * 3,
        scratch_shapes=[pltpu.VMEM((2 * block[0], block[1]), F32)],
        compiler_params=params(12),
        cost_estimate=LITTLE,
        name="ring_total",
    )(me, *[held(a) for a in (later, below0, above0, below1, above1)])


def add_up(*groups):
    flat = [a for g in groups for a in g]

    def body(*refs):
        at = 0
        for g, out_ref in zip(groups, refs[len(flat) :]):
            total = refs[at][...].astype(F32)
            for ref in refs[at + 1 : at + len(g)]:
                total += ref[...].astype(F32)
            out_ref[...] = total
            at += len(g)

    return pl.pallas_call(
        body,
        in_specs=[IN_VMEM] * len(flat),
        out_specs=[IN_VMEM] * len(groups),
        out_shape=[jax.ShapeDtypeStruct(g[0].shape, F32) for g in groups],
        compiler_params=params(10),
        cost_estimate=LITTLE,
        name="add_up",
    )(*[held(a) for a in flat])


def after(values, *deps):
    return lax.optimization_barrier((values, deps))[0]


def on_device(tokens, picks, counts, score, w_in, w_out, cotan):
    routed = picks.shape[0]
    n_tok = tokens.shape[0]

    own_mine, me = take_rows(tokens, picks, counts, score, cotan)
    w_in, w_out = hold(*after((w_in, w_out), own_mine))
    near_mine = move_lane(own_mine, 1)
    own_other = swap_core(own_mine)
    own = hidden_units([[own_mine], [own_other]], w_in, w_out)

    near_other = move_lane(own_other, 1)
    near_mine = after(near_mine, own)
    far_mine = move_lane(near_mine, 1)
    swapped_mine = [swap_core(near_mine[:1]), swap_core(near_mine[1:])]
    own_terms = row_terms(own[0], own[1], w_in, w_out, routed, 1)
    own_got = swap_core(own_terms[1])
    near_mine, swapped_mine = after((near_mine, swapped_mine), own_terms)
    near = hidden_units([[near_mine], swapped_mine], w_in, w_out)
    near_terms = row_terms(near[0], near[1], w_in, w_out, routed, 3)

    near_other = after(near_other, near)
    swapped_other = [swap_core(near_other[:1]), swap_core(near_other[1:])]
    swapped_other, own_got = after((swapped_other, own_got), near_terms)
    other = hidden_units([[near_other], swapped_other], w_in, w_out)
    near_terms = row_terms(other[0], other[1], w_in, w_out, routed, 3, 1, near_terms)

    far_mine = after(far_mine, other)
    far_packs = after([far_mine, swap_core(far_mine)], near_terms)
    far = hidden_units([[p] for p in far_packs], w_in, w_out, True)
    last_terms = row_terms(far[0], far[1], w_in, w_out, routed, 3, 2, near_terms, True)
    last_got = swap_core(last_terms[1])

    all_packs = [own_mine, own_other, near_mine, swapped_mine[0], near_other, swapped_other[0]] + far_packs
    hidden, dpre, turned = ([u[i] for u in (own, near, other, far)] for i in range(3))
    all_packs, dpre = after((all_packs, dpre), last_terms)
    in_up, in_down = in_blocks(me, all_packs, dpre, FIRST_STEP)
    in_below, in_above = move_x(in_up, 1), move_x(in_down, -1)

    hidden, turned = after((hidden, turned), in_up, in_down)
    out_up, out_down = out_blocks(me, hidden, turned, FIRST_STEP)
    out_below, out_above = move_y(out_up, 1), move_y(out_down, -1)

    last_got = after(last_got, out_up, out_down)
    to_far = (last_terms[0][2].astype(F32) + last_got[2].astype(F32)).astype(BF16)
    z_far = move_lane(to_far, -1)
    all_packs, dpre = after((all_packs, dpre), to_far)
    in_later = in_blocks(me, all_packs, dpre, LATER_STEP)[0]
    z_far = after(z_far, in_later)
    passed = jnp.pad(z_far.astype(F32)[None], ((0, 1), (0, 0), (0, 0), (0, 0)))
    to_near = (last_terms[0][:2].astype(F32) + last_got[:2].astype(F32) + passed).astype(BF16)
    z_near = move_lane(to_near, -1)
    hidden, turned = after((hidden, turned), to_near)
    out_later = out_blocks(me, hidden, turned, LATER_STEP)[0]

    def second_hop(later, from_below, from_above, move):
        up = (later[0].astype(F32) + from_below[0].astype(F32)).astype(BF16)
        down = (later[1].astype(F32) + from_above[0].astype(F32)).astype(BF16)
        return move(up, 1), move(down, -1), up, down

    in_below, in_above, out_below, out_above = after((in_below, in_above, out_below, out_above), out_later)
    in_hops = second_hop(in_later, in_below, in_above, move_x)
    out_hops = second_hop(out_later, out_below, out_above, move_y)
    in_total = ring_total(me, in_later, in_hops[0], in_above, in_below, in_hops[1], True)
    out_hops = after(out_hops[:2], in_total)
    z_near = after(z_near, in_total, out_hops)
    z_other = swap_core(z_near[1])

    def second_stage(total, move):
        keep, following, previous, far = total
        return keep, move(far, 2), move(following, 1), move(previous, -1)

    out_total = ring_total(me, out_later, out_hops[0], out_above, out_below, out_hops[1], False)
    in_total, out_total = after((in_total, out_total), z_other)
    in_parts = second_stage(in_total, move_y)
    out_parts = second_stage(out_total, move_x)

    back = (
        own_terms[0][0].astype(F32) + own_got[0].astype(F32) + z_near[0].astype(F32) + z_other.astype(F32)
    ).astype(BF16)
    ffn = back[0].astype(F32)
    heavy = (score[:, None] * ffn).astype(BF16)
    grad_score = jnp.sum(cotan.astype(F32) * ffn, axis=1)
    place = picks[:, None] == jnp.arange(n_tok, dtype=jnp.int32)[None, :]
    grad_x = dot(place.astype(BF16), back[1], ((0,), (0,))).astype(BF16)
    in_parts, out_parts = after((in_parts, out_parts), heavy, grad_x)
    grad_in, grad_out = add_up(in_parts, out_parts)
    return (heavy, grad_x, grad_score, grad_in, grad_out)


def solution(mesh):
    placed = (
        P(("ctx", "head"), None),
        P(("ctx", "head")),
        P(("ctx", "head")),
        P(("ctx", "head")),
        P(None, "head"),
        P("head", None),
        P(("ctx", "head"), None),
    )
    return jax.shard_map(
        on_device,
        mesh=mesh,
        in_specs=placed,
        out_specs=(
            P(("ctx", "head"), None),
            P(("ctx", "head"), None),
            P(("ctx", "head")),
            P("ctx", "head"),
            P("head", "ctx"),
        ),
        check_vma=False,
    )
```

```python
import functools

import jax
import jax.numpy as jnp
from jax import lax
from jax.experimental import pallas as pl
from jax.experimental.pallas import tpu as pltpu
from jax.sharding import PartitionSpec as P

F32 = jnp.float32
BF16 = jnp.bfloat16
SIDE = 4
MIB = 1024 * 1024
LITTLE = pl.CostEstimate(flops=1, bytes_accessed=1, transcendentals=0)
IN_VMEM = pl.BlockSpec(memory_space=pltpu.VMEM)
IN_SMEM = pl.BlockSpec(memory_space=pltpu.SMEM)


def gelu_parts(u):
    c = 0.7978845608
    t = jnp.tanh(c * (u + 0.044715 * u * u * u))
    value = 0.5 * u * (1.0 + t)
    slope = 0.5 * (1.0 + t) + 0.5 * u * (1.0 - t * t) * c * (1.0 + 3.0 * 0.044715 * u * u)
    return (value, slope)


def move_x(v, by):
    perm = [(x * SIDE + y, ((x + by) % SIDE) * SIDE + y) for x in range(SIDE) for y in range(SIDE)]
    return lax.ppermute(v, "ctx", perm)


def move_y(v, by):
    perm = [(x * SIDE + y, x * SIDE + (y + by) % SIDE) for x in range(SIDE) for y in range(SIDE)]
    return lax.ppermute(v, "ctx", perm)


def move_lane(v, by):
    perm = [(z * 2 + c, ((z + (by if c == 0 else -by)) % SIDE) * 2 + c) for z in range(SIDE) for c in range(2)]
    return lax.ppermute(v, "head", perm)


def swap_core(v):
    return lax.ppermute(v, "head", [(i, i ^ 1) for i in range(2 * SIDE)])


def dot(a, b, dims):
    return lax.dot_general(a, b, ((dims[0], dims[1]), ((), ())), preferred_element_type=F32)


def params(mib):
    return pltpu.CompilerParams(vmem_limit_bytes=mib * MIB)


def whole(a):
    return pl.BlockSpec(a.shape, lambda *_: (0,) * a.ndim)


def take_rows(tokens, picks, counts, score, cotan):
    routed = picks.shape[0]
    n_tok, width = tokens.shape
    parts = 2
    part = width // parts

    def body(counts_ref, picks_hbm, score_hbm, tokens_ref, cotan_ref, out_ref, me_ref, *scratch):
        rows_in, cotan_in, picks_ref, score_ref, sems = scratch
        small = [
            pltpu.make_async_copy(picks_hbm, picks_ref, sems.at[parts + 1]),
            pltpu.make_async_copy(score_hbm, score_ref, sems.at[parts + 2]),
        ]
        for copy in small:
            copy.start()
        copies = [pltpu.make_async_copy(cotan_ref, cotan_in, sems.at[parts])]
        for p in range(parts):
            cols = pl.ds(p * part, part)
            copies.append(pltpu.make_async_copy(tokens_ref.at[:, cols], rows_in.at[p], sems.at[p]))
        for copy in copies:
            copy.start()
        me_ref[0] = lax.axis_index("ctx").astype(jnp.int32)
        me_ref[1] = lax.axis_index("head").astype(jnp.int32)
        for copy in small:
            copy.wait()
        places = lax.broadcasted_iota(jnp.int32, (n_tok, routed), 0)
        slots = lax.broadcasted_iota(jnp.int32, (n_tok, routed), 1)
        hit = (places == picks_ref[...]) & (slots < counts_ref[0])
        one_hot = jnp.where(hit, 1.0, 0.0).astype(BF16)
        across = lax.broadcasted_iota(jnp.int32, (routed, routed), 0)
        along = lax.broadcasted_iota(jnp.int32, (routed, routed), 1)
        kept = (across == along) & (along < counts_ref[0])
        factor = jnp.sum(jnp.where(kept, score_ref[...], 0.0), axis=1, keepdims=True)
        copies[0].wait()
        out_ref[1] = (factor * cotan_in[...].astype(F32)).astype(BF16)
        for p in range(parts):
            copies[1 + p].wait()
            out_ref[0, :, pl.ds(p * part, part)] = dot(one_hot, rows_in[p], ((0,), (0,))).astype(BF16)

    in_hbm = pl.BlockSpec(memory_space=pl.ANY)
    return pl.pallas_call(
        body,
        in_specs=[IN_SMEM] + [in_hbm] * 4,
        out_specs=[IN_VMEM, IN_SMEM],
        out_shape=[pltpu.VMEM((2, routed, width), BF16), jax.ShapeDtypeStruct((2,), jnp.int32)],
        scratch_shapes=[
            pltpu.VMEM((parts, n_tok, part), BF16),
            pltpu.VMEM((routed, width), BF16),
            pltpu.VMEM((1, routed), jnp.int32),
            pltpu.VMEM((1, routed), F32),
            pltpu.SemaphoreType.DMA((parts + 3,)),
        ],
        compiler_params=params(12),
        cost_estimate=LITTLE,
        name="take_rows",
    )(
        counts,
        *[pltpu.with_memory_space_constraint(a, pltpu.HBM) for a in (picks[None, :], score[None, :], tokens, cotan)],
    )


def held(a):
    return pltpu.with_memory_space_constraint(a, pltpu.VMEM)


def on_held(body, arrays, shapes, name, me=None, spare=(), aliases={}):
    first = [] if me is None else [me]
    return pl.pallas_call(
        body,
        in_specs=[IN_SMEM] * len(first) + [IN_VMEM] * len(arrays) + [pl.BlockSpec(memory_space=pl.ANY)] * len(spare),
        out_specs=[IN_VMEM] * len(shapes),
        out_shape=[pltpu.VMEM(shape, dtype) for shape, dtype in shapes],
        input_output_aliases=aliases,
        compiler_params=params(12),
        cost_estimate=LITTLE,
        name=name,
    )(*first, *[held(a) for a in arrays], *[held(a) for a in spare])


def repeat(count, step, unrolled):
    if unrolled:
        for i in range(count):
            step(i)
    else:
        lax.fori_loop(0, count, lambda i, c: (step(i), c)[1], 0)


def span(i, size):
    at = i * size
    return pl.ds(at if isinstance(i, int) else pl.multiple_of(at, size), size)


def hidden_units(packs, w_in, w_out, unrolled=False):
    halves = [(i, h) for i, p in enumerate(packs) for h in range(len(p))]
    at = {p: k for k, p in enumerate(halves)}
    where_r = [at[(i, 0)] for i in range(len(packs))]
    where_d = [at[(i, len(p) - 1)] for i, p in enumerate(packs)]
    flat = [a for p in packs for a in p]
    n = len(packs)
    _, piece, width = flat[0].shape
    count = n * piece
    hid = w_in.shape[1]
    tile = hid // SIDE
    quarter = width // SIDE
    strip = quarter // SIDE

    def body(*refs):
        last = [refs[k].shape[0] - 1 for k in where_d]
        r = jnp.concatenate([refs[k][0] for k in where_r], axis=0)
        d = jnp.concatenate([refs[k][i] for k, i in zip(where_d, last)], axis=0)
        win_ref, wout_ref, hidden_ref, dpre_ref, turned_ref = refs[len(flat) :]

        def step(j):
            cols = span(j, tile)
            pre = dot(r, win_ref[:, cols], ((1,), (0,)))
            dhid = dot(d, wout_ref[cols, :], ((1,), (1,)))
            value, slope = gelu_parts(pre)
            hidden_ref[:, cols] = value.astype(BF16)
            dpre_ref[:, cols] = (dhid * slope).astype(BF16)
            for x in range(SIDE):
                to = span(j * SIDE + x, strip)
                for k in range(n):
                    turned_ref[pl.ds(k * piece, piece), to] = refs[where_d[k]][last[k], :, span(x * SIDE + j, strip)]

        repeat(SIDE, step, unrolled)

    shapes = [((count, hid), BF16), ((count, hid), BF16), ((count, width), BF16)]
    return on_held(body, flat + [w_in, w_out], shapes, "hidden_units")


def hold(w_in, w_out):
    def body(win_ref, wout_ref, win_out, wout_out, sems):
        copies = [
            pltpu.make_async_copy(win_ref, win_out, sems.at[0]),
            pltpu.make_async_copy(wout_ref, wout_out, sems.at[1]),
        ]
        for copy in copies:
            copy.start()
        for copy in copies:
            copy.wait()

    return pl.pallas_call(
        body,
        in_specs=[pl.BlockSpec(memory_space=pl.ANY)] * 2,
        out_specs=[pl.BlockSpec(memory_space=pltpu.VMEM)] * 2,
        out_shape=[pltpu.VMEM(w.shape, w.dtype) for w in (w_in, w_out)],
        scratch_shapes=[pltpu.SemaphoreType.DMA((2,))],
        compiler_params=params(4),
        cost_estimate=LITTLE,
        name="hold_weights",
    )(pltpu.with_memory_space_constraint(w_in, pltpu.HBM), pltpu.with_memory_space_constraint(w_out, pltpu.HBM))


def row_terms(hidden, dpre, w_in, w_out, piece, groups, first=0, held_terms=(), unrolled=False):
    count, hid = hidden.shape
    width = w_in.shape[0]
    n = count // (2 * piece)
    tile = width // SIDE

    def body(hidden_ref, dpre_ref, win_ref, wout_ref, *refs):
        outs = refs[len(held_terms) :]

        def step(j):
            cols = span(j, tile)
            ffn = dot(hidden_ref[...], wout_ref[:, cols], ((1,), (0,))).astype(BF16)
            dx = dot(dpre_ref[...], win_ref[cols, :], ((1,), (1,))).astype(BF16)
            for h in range(2):
                for k in range(n):
                    for s, v in enumerate((ffn, dx)):
                        outs[h][first + k, s, :, cols] = v[(h * n + k) * piece : (h * n + k + 1) * piece]

        repeat(SIDE, step, unrolled)

    shapes = [((groups, 2, piece, width), BF16)] * 2
    aliases = {4 + i: i for i in range(len(held_terms))}
    return on_held(body, [hidden, dpre, w_in, w_out], shapes, "row_terms", spare=held_terms, aliases=aliases)


FIRST_STEP = ((2, 0), (2, 1), (1, 1), (3, 0))
LATER_STEP = ((1, 0), (3, 1), (0, 0), (0, 1))


def make_blocks(steps, outs, make):
    if steps is FIRST_STEP:
        for i, (place, half) in enumerate(steps):
            outs[i % 2][i // 2] = make(place, half).astype(BF16)
    else:

        def step(i):
            place = jnp.where(i >= 2, 0, jnp.where(i == 0, 1, 3))
            half = jnp.where((i == 1) | (i == 3), 1, 0)
            outs[0][i] = make(place, half).astype(BF16)

        repeat(len(steps), step, False)


def block_shapes(steps, block):
    return [((2,) + block, BF16)] * 2 if steps is FIRST_STEP else [((len(steps),) + block, BF16)]


def in_blocks(me, packs, dpre, steps):
    n = len(packs)
    _, piece, width = packs[0].shape
    hid = dpre[0].shape[1]
    size = width // (2 * SIDE)
    each = n // len(dpre)

    def body(me_ref, *refs):
        def make(place, half):
            to = 2 * lax.rem(me_ref[0] // SIDE + place, SIDE) + half
            cols = pl.ds(pl.multiple_of(to * size, size), size)
            term = None
            for c in range(len(dpre)):
                r = jnp.concatenate([ref[0, :, cols] for ref in refs[c * each : (c + 1) * each]], axis=0)
                part = dot(r, refs[n + c][...], ((0,), (0,)))
                term = part if term is None else term + part
            return term

        make_blocks(steps, refs[n + len(dpre) :], make)

    return on_held(body, packs + dpre, block_shapes(steps, (size, hid)), "in_blocks", me)


def out_blocks(me, hidden, turned, steps):
    n = len(hidden)
    hid = hidden[0].shape[1]
    quarter = turned[0].shape[1] // SIDE

    def body(me_ref, *refs):
        def make(place, half):
            to = lax.rem(lax.rem(me_ref[0], SIDE) + place, SIDE)
            cols = pl.ds(pl.multiple_of(to * quarter, quarter), quarter)
            term = None
            for c in range(n):
                part = dot(refs[c][:, span(half, hid // 2)], refs[n + c][:, cols], ((0,), (0,)))
                term = part if term is None else term + part
            return term

        make_blocks(steps, refs[2 * n :], make)

    return on_held(body, hidden + turned, block_shapes(steps, (hid // 2, quarter)), "out_blocks", me)


def ring_total(me, later, below0, above0, below1, above1, rowwise):
    block = later.shape[1:]
    if rowwise:
        cut = (2 * block[0] // SIDE, block[1])
    else:
        cut = (2 * block[0], block[1] // SIDE)

    def body(me_ref, later_ref, b0, a0, b1, a1, keep_ref, next_ref, prev_ref, far_ref, sum_ref):
        half = block[0]
        rows = half // SIDE

        def step(j):
            cut_j = span(j, rows)
            first = later_ref[2, cut_j].astype(F32) + b0[cut_j].astype(F32) + a0[1, cut_j].astype(F32)
            second = later_ref[3, cut_j].astype(F32) + b1[1, cut_j].astype(F32) + a1[cut_j].astype(F32)
            sum_ref[cut_j, :] = first
            sum_ref[span(j + SIDE, rows), :] = second

        repeat(SIDE, step, False)
        if rowwise:
            at = lax.rem(me_ref[0], SIDE)
        else:
            at = me_ref[0] // SIDE
        for k, ref in ((0, keep_ref), (1, next_ref), (3, prev_ref), (2, far_ref)):
            to = lax.rem(at + k, SIDE)
            if rowwise:
                v = sum_ref[pl.ds(pl.multiple_of(to * cut[0], cut[0]), cut[0]), :]
            else:
                v = sum_ref[:, pl.ds(pl.multiple_of(to * cut[1], cut[1]), cut[1])]
            ref[...] = v.astype(ref.dtype)

    return pl.pallas_call(
        body,
        in_specs=[IN_SMEM] + [IN_VMEM] * 5,
        out_specs=[IN_VMEM] * 4,
        out_shape=[pltpu.VMEM(cut, F32)] + [pltpu.VMEM(cut, BF16)] * 3,
        scratch_shapes=[pltpu.VMEM((2 * block[0], block[1]), F32)],
        compiler_params=params(12),
        cost_estimate=LITTLE,
        name="ring_total",
    )(me, *[held(a) for a in (later, below0, above0, below1, above1)])


def add_up(*groups):
    flat = [a for g in groups for a in g]

    def body(*refs):
        at = 0
        for g, out_ref in zip(groups, refs[len(flat) :]):
            total = refs[at][...].astype(F32)
            for ref in refs[at + 1 : at + len(g)]:
                total += ref[...].astype(F32)
            out_ref[...] = total
            at += len(g)

    return pl.pallas_call(
        body,
        in_specs=[IN_VMEM] * len(flat),
        out_specs=[IN_VMEM] * len(groups),
        out_shape=[jax.ShapeDtypeStruct(g[0].shape, F32) for g in groups],
        compiler_params=params(10),
        cost_estimate=LITTLE,
        name="add_up",
    )(*[held(a) for a in flat])


def after(values, *deps):
    return lax.optimization_barrier((values, deps))[0]


def on_device(tokens, picks, counts, score, w_in, w_out, cotan):
    routed = picks.shape[0]
    n_tok = tokens.shape[0]

    own_mine, me = take_rows(tokens, picks, counts, score, cotan)
    w_in, w_out = hold(*after((w_in, w_out), own_mine))
    near_mine = move_lane(own_mine, 1)
    own_other = swap_core(own_mine)
    own = hidden_units([[own_mine], [own_other]], w_in, w_out)

    near_other = move_lane(own_other, 1)
    near_mine = after(near_mine, own)
    far_mine = move_lane(near_mine, 1)
    swapped_mine = [swap_core(near_mine[:1]), swap_core(near_mine[1:])]
    own_terms = row_terms(own[0], own[1], w_in, w_out, routed, 1)
    own_got = swap_core(own_terms[1])
    near_mine, swapped_mine = after((near_mine, swapped_mine), own_terms)
    near = hidden_units([[near_mine], swapped_mine], w_in, w_out)
    near_terms = row_terms(near[0], near[1], w_in, w_out, routed, 3)

    near_other = after(near_other, near)
    swapped_other = [swap_core(near_other[:1]), swap_core(near_other[1:])]
    swapped_other, own_got = after((swapped_other, own_got), near_terms)
    other = hidden_units([[near_other], swapped_other], w_in, w_out)
    near_terms = row_terms(other[0], other[1], w_in, w_out, routed, 3, 1, near_terms)

    far_mine = after(far_mine, near_terms)
    far_packs = [far_mine, swap_core(far_mine)]
    far = hidden_units([[p] for p in far_packs], w_in, w_out, True)
    last_terms = row_terms(far[0], far[1], w_in, w_out, routed, 3, 2, near_terms, True)
    last_got = swap_core(last_terms[1])

    all_packs = [own_mine, own_other, near_mine, swapped_mine[0], near_other, swapped_other[0]] + far_packs
    hidden, dpre, turned = ([u[i] for u in (own, near, other, far)] for i in range(3))
    all_packs, dpre = after((all_packs, dpre), last_terms)
    in_up, in_down = in_blocks(me, all_packs, dpre, FIRST_STEP)
    in_below, in_above = move_x(in_up, 1), move_x(in_down, -1)

    hidden, turned = after((hidden, turned), in_up, in_down)
    out_up, out_down = out_blocks(me, hidden, turned, FIRST_STEP)
    out_below, out_above = move_y(out_up, 1), move_y(out_down, -1)

    last_got = after(last_got, out_up, out_down)
    to_far = (last_terms[0][2].astype(F32) + last_got[2].astype(F32)).astype(BF16)
    z_far = move_lane(to_far, -1)
    all_packs, dpre = after((all_packs, dpre), to_far)
    in_later = in_blocks(me, all_packs, dpre, LATER_STEP)[0]
    z_far = after(z_far, in_later)
    passed = jnp.pad(z_far.astype(F32)[None], ((0, 1), (0, 0), (0, 0), (0, 0)))
    to_near = (last_terms[0][:2].astype(F32) + last_got[:2].astype(F32) + passed).astype(BF16)
    z_near = move_lane(to_near, -1)
    hidden, turned = after((hidden, turned), to_near)
    out_later = out_blocks(me, hidden, turned, LATER_STEP)[0]

    def second_hop(later, from_below, from_above, move):
        up = (later[0].astype(F32) + from_below[0].astype(F32)).astype(BF16)
        down = (later[1].astype(F32) + from_above[0].astype(F32)).astype(BF16)
        return move(up, 1), move(down, -1), up, down

    in_below, in_above, out_below, out_above = after((in_below, in_above, out_below, out_above), out_later)
    in_hops = second_hop(in_later, in_below, in_above, move_x)
    out_hops = second_hop(out_later, out_below, out_above, move_y)
    in_total = ring_total(me, in_later, in_hops[0], in_above, in_below, in_hops[1], True)
    out_hops = after(out_hops[:2], in_total)
    z_near = after(z_near, in_total, out_hops)
    z_other = swap_core(z_near[1])

    def second_stage(total, move):
        keep, following, previous, far = total
        return keep, move(far, 2), move(following, 1), move(previous, -1)

    out_total = ring_total(me, out_later, out_hops[0], out_above, out_below, out_hops[1], False)
    in_total, out_total = after((in_total, out_total), z_other)
    in_parts = second_stage(in_total, move_y)
    out_parts = second_stage(out_total, move_x)

    back = (
        own_terms[0][0].astype(F32) + own_got[0].astype(F32) + z_near[0].astype(F32) + z_other.astype(F32)
    ).astype(BF16)
    ffn = back[0].astype(F32)
    heavy = (score[:, None] * ffn).astype(BF16)
    grad_score = jnp.sum(cotan.astype(F32) * ffn, axis=1)
    place = picks[:, None] == jnp.arange(n_tok, dtype=jnp.int32)[None, :]
    grad_x = dot(place.astype(BF16), back[1], ((0,), (0,))).astype(BF16)
    in_parts, out_parts = after((in_parts, out_parts), heavy, grad_x)
    grad_in, grad_out = add_up(in_parts, out_parts)
    return (heavy, grad_x, grad_score, grad_in, grad_out)


def solution(mesh):
    placed = (
        P(("ctx", "head"), None),
        P(("ctx", "head")),
        P(("ctx", "head")),
        P(("ctx", "head")),
        P(None, "head"),
        P("head", None),
        P(("ctx", "head"), None),
    )
    return jax.shard_map(
        on_device,
        mesh=mesh,
        in_specs=placed,
        out_specs=(
            P(("ctx", "head"), None),
            P(("ctx", "head"), None),
            P(("ctx", "head")),
            P("ctx", "head"),
            P("head", "ctx"),
        ),
        check_vma=False,
    )
```

```python
import functools

import jax
import jax.numpy as jnp
from jax import lax
from jax.experimental import pallas as pl
from jax.experimental.pallas import tpu as pltpu
from jax.sharding import PartitionSpec as P

F32 = jnp.float32
BF16 = jnp.bfloat16
SIDE = 4
MIB = 1024 * 1024
LITTLE = pl.CostEstimate(flops=1, bytes_accessed=1, transcendentals=0)
IN_VMEM = pl.BlockSpec(memory_space=pltpu.VMEM)
IN_SMEM = pl.BlockSpec(memory_space=pltpu.SMEM)


def gelu_parts(u):
    c = 0.7978845608
    t = jnp.tanh(c * (u + 0.044715 * u * u * u))
    value = 0.5 * u * (1.0 + t)
    slope = 0.5 * (1.0 + t) + 0.5 * u * (1.0 - t * t) * c * (1.0 + 3.0 * 0.044715 * u * u)
    return (value, slope)


def move_x(v, by):
    perm = [(x * SIDE + y, ((x + by) % SIDE) * SIDE + y) for x in range(SIDE) for y in range(SIDE)]
    return lax.ppermute(v, "ctx", perm)


def move_y(v, by):
    perm = [(x * SIDE + y, x * SIDE + (y + by) % SIDE) for x in range(SIDE) for y in range(SIDE)]
    return lax.ppermute(v, "ctx", perm)


def move_lane(v, by):
    perm = [(z * 2 + c, ((z + (by if c == 0 else -by)) % SIDE) * 2 + c) for z in range(SIDE) for c in range(2)]
    return lax.ppermute(v, "head", perm)


def swap_core(v):
    return lax.ppermute(v, "head", [(i, i ^ 1) for i in range(2 * SIDE)])


def dot(a, b, dims):
    return lax.dot_general(a, b, ((dims[0], dims[1]), ((), ())), preferred_element_type=F32)


def params(mib):
    return pltpu.CompilerParams(vmem_limit_bytes=mib * MIB)


def whole(a):
    return pl.BlockSpec(a.shape, lambda *_: (0,) * a.ndim)


def take_rows(tokens, picks, counts, score, cotan):
    routed = picks.shape[0]
    n_tok, width = tokens.shape
    parts = 2
    part = width // parts

    def body(counts_ref, picks_hbm, score_hbm, tokens_ref, cotan_ref, out_ref, me_ref, *scratch):
        rows_in, cotan_in, picks_ref, score_ref, sems = scratch
        small = [
            pltpu.make_async_copy(picks_hbm, picks_ref, sems.at[parts + 1]),
            pltpu.make_async_copy(score_hbm, score_ref, sems.at[parts + 2]),
        ]
        for copy in small:
            copy.start()
        copies = [pltpu.make_async_copy(cotan_ref, cotan_in, sems.at[parts])]
        for p in range(parts):
            cols = pl.ds(p * part, part)
            copies.append(pltpu.make_async_copy(tokens_ref.at[:, cols], rows_in.at[p], sems.at[p]))
        for copy in copies:
            copy.start()
        me_ref[0] = lax.axis_index("ctx").astype(jnp.int32)
        me_ref[1] = lax.axis_index("head").astype(jnp.int32)
        for copy in small:
            copy.wait()
        places = lax.broadcasted_iota(jnp.int32, (n_tok, routed), 0)
        slots = lax.broadcasted_iota(jnp.int32, (n_tok, routed), 1)
        hit = (places == picks_ref[...]) & (slots < counts_ref[0])
        one_hot = jnp.where(hit, 1.0, 0.0).astype(BF16)
        across = lax.broadcasted_iota(jnp.int32, (routed, routed), 0)
        along = lax.broadcasted_iota(jnp.int32, (routed, routed), 1)
        kept = (across == along) & (along < counts_ref[0])
        factor = jnp.sum(jnp.where(kept, score_ref[...], 0.0), axis=1, keepdims=True)
        copies[0].wait()
        out_ref[1] = (factor * cotan_in[...].astype(F32)).astype(BF16)
        for p in range(parts):
            copies[1 + p].wait()
            out_ref[0, :, pl.ds(p * part, part)] = dot(one_hot, rows_in[p], ((0,), (0,))).astype(BF16)

    in_hbm = pl.BlockSpec(memory_space=pl.ANY)
    return pl.pallas_call(
        body,
        in_specs=[IN_SMEM] + [in_hbm] * 4,
        out_specs=[IN_VMEM, IN_SMEM],
        out_shape=[pltpu.VMEM((2, routed, width), BF16), jax.ShapeDtypeStruct((2,), jnp.int32)],
        scratch_shapes=[
            pltpu.VMEM((parts, n_tok, part), BF16),
            pltpu.VMEM((routed, width), BF16),
            pltpu.VMEM((1, routed), jnp.int32),
            pltpu.VMEM((1, routed), F32),
            pltpu.SemaphoreType.DMA((parts + 3,)),
        ],
        compiler_params=params(12),
        cost_estimate=LITTLE,
        name="take_rows",
    )(
        counts,
        *[pltpu.with_memory_space_constraint(a, pltpu.HBM) for a in (picks[None, :], score[None, :], tokens, cotan)],
    )


def held(a):
    return pltpu.with_memory_space_constraint(a, pltpu.VMEM)


def on_held(body, arrays, shapes, name, me=None, spare=(), aliases={}):
    first = [] if me is None else [me]
    return pl.pallas_call(
        body,
        in_specs=[IN_SMEM] * len(first) + [IN_VMEM] * len(arrays) + [pl.BlockSpec(memory_space=pl.ANY)] * len(spare),
        out_specs=[IN_VMEM] * len(shapes),
        out_shape=[pltpu.VMEM(shape, dtype) for shape, dtype in shapes],
        input_output_aliases=aliases,
        compiler_params=params(12),
        cost_estimate=LITTLE,
        name=name,
    )(*first, *[held(a) for a in arrays], *[held(a) for a in spare])


def repeat(count, step, unrolled):
    if unrolled:
        for i in range(count):
            step(i)
    else:
        lax.fori_loop(0, count, lambda i, c: (step(i), c)[1], 0)


def span(i, size):
    at = i * size
    return pl.ds(at if isinstance(i, int) else pl.multiple_of(at, size), size)


def hidden_units(packs, w_in, w_out, unrolled=False):
    halves = [(i, h) for i, p in enumerate(packs) for h in range(len(p))]
    at = {p: k for k, p in enumerate(halves)}
    where_r = [at[(i, 0)] for i in range(len(packs))]
    where_d = [at[(i, len(p) - 1)] for i, p in enumerate(packs)]
    flat = [a for p in packs for a in p]
    n = len(packs)
    _, piece, width = flat[0].shape
    count = n * piece
    hid = w_in.shape[1]
    tile = hid // SIDE
    quarter = width // SIDE
    strip = quarter // SIDE

    def body(*refs):
        last = [refs[k].shape[0] - 1 for k in where_d]
        r = jnp.concatenate([refs[k][0] for k in where_r], axis=0)
        d = jnp.concatenate([refs[k][i] for k, i in zip(where_d, last)], axis=0)
        win_ref, wout_ref, hidden_ref, dpre_ref, turned_ref = refs[len(flat) :]

        def step(j):
            cols = span(j, tile)
            pre = dot(r, win_ref[:, cols], ((1,), (0,)))
            dhid = dot(d, wout_ref[cols, :], ((1,), (1,)))
            value, slope = gelu_parts(pre)
            hidden_ref[:, cols] = value.astype(BF16)
            dpre_ref[:, cols] = (dhid * slope).astype(BF16)
            for x in range(SIDE):
                to = span(j * SIDE + x, strip)
                for k in range(n):
                    turned_ref[pl.ds(k * piece, piece), to] = refs[where_d[k]][last[k], :, span(x * SIDE + j, strip)]

        repeat(SIDE, step, unrolled)

    shapes = [((count, hid), BF16), ((count, hid), BF16), ((count, width), BF16)]
    return on_held(body, flat + [w_in, w_out], shapes, "hidden_units")


def hold(w_in, w_out):
    def body(win_ref, wout_ref, win_out, wout_out, sems):
        copies = [
            pltpu.make_async_copy(win_ref, win_out, sems.at[0]),
            pltpu.make_async_copy(wout_ref, wout_out, sems.at[1]),
        ]
        for copy in copies:
            copy.start()
        for copy in copies:
            copy.wait()

    return pl.pallas_call(
        body,
        in_specs=[pl.BlockSpec(memory_space=pl.ANY)] * 2,
        out_specs=[pl.BlockSpec(memory_space=pltpu.VMEM)] * 2,
        out_shape=[pltpu.VMEM(w.shape, w.dtype) for w in (w_in, w_out)],
        scratch_shapes=[pltpu.SemaphoreType.DMA((2,))],
        compiler_params=params(4),
        cost_estimate=LITTLE,
        name="hold_weights",
    )(pltpu.with_memory_space_constraint(w_in, pltpu.HBM), pltpu.with_memory_space_constraint(w_out, pltpu.HBM))


def row_terms(hidden, dpre, w_in, w_out, piece, groups, first=0, held_terms=(), unrolled=False):
    count, hid = hidden.shape
    width = w_in.shape[0]
    n = count // (2 * piece)
    tile = width // SIDE

    def body(hidden_ref, dpre_ref, win_ref, wout_ref, *refs):
        outs = refs[len(held_terms) :]

        def step(j):
            cols = span(j, tile)
            ffn = dot(hidden_ref[...], wout_ref[:, cols], ((1,), (0,))).astype(BF16)
            dx = dot(dpre_ref[...], win_ref[cols, :], ((1,), (1,))).astype(BF16)
            for h in range(2):
                for k in range(n):
                    for s, v in enumerate((ffn, dx)):
                        outs[h][first + k, s, :, cols] = v[(h * n + k) * piece : (h * n + k + 1) * piece]

        repeat(SIDE, step, unrolled)

    shapes = [((groups, 2, piece, width), BF16)] * 2
    aliases = {4 + i: i for i in range(len(held_terms))}
    return on_held(body, [hidden, dpre, w_in, w_out], shapes, "row_terms", spare=held_terms, aliases=aliases)


FIRST_STEP = ((2, 0), (2, 1), (1, 1), (3, 0))
LATER_STEP = ((1, 0), (3, 1), (0, 0), (0, 1))


def make_blocks(steps, outs, make):
    if steps is FIRST_STEP:
        for i, (place, half) in enumerate(steps):
            outs[i % 2][i // 2] = make(place, half).astype(BF16)
    else:

        def step(i):
            place = jnp.where(i >= 2, 0, jnp.where(i == 0, 1, 3))
            half = jnp.where((i == 1) | (i == 3), 1, 0)
            outs[0][i] = make(place, half).astype(BF16)

        repeat(len(steps), step, False)


def block_shapes(steps, block):
    return [((2,) + block, BF16)] * 2 if steps is FIRST_STEP else [((len(steps),) + block, BF16)]


def in_blocks(me, packs, dpre, steps):
    n = len(packs)
    _, piece, width = packs[0].shape
    hid = dpre[0].shape[1]
    size = width // (2 * SIDE)
    each = n // len(dpre)

    def body(me_ref, *refs):
        def make(place, half):
            to = 2 * lax.rem(me_ref[0] // SIDE + place, SIDE) + half
            cols = pl.ds(pl.multiple_of(to * size, size), size)
            term = None
            for c in range(len(dpre)):
                r = jnp.concatenate([ref[0, :, cols] for ref in refs[c * each : (c + 1) * each]], axis=0)
                part = dot(r, refs[n + c][...], ((0,), (0,)))
                term = part if term is None else term + part
            return term

        make_blocks(steps, refs[n + len(dpre) :], make)

    return on_held(body, packs + dpre, block_shapes(steps, (size, hid)), "in_blocks", me)


def out_blocks(me, hidden, turned, steps):
    n = len(hidden)
    hid = hidden[0].shape[1]
    quarter = turned[0].shape[1] // SIDE

    def body(me_ref, *refs):
        def make(place, half):
            to = lax.rem(lax.rem(me_ref[0], SIDE) + place, SIDE)
            cols = pl.ds(pl.multiple_of(to * quarter, quarter), quarter)
            term = None
            for c in range(n):
                part = dot(refs[c][:, span(half, hid // 2)], refs[n + c][:, cols], ((0,), (0,)))
                term = part if term is None else term + part
            return term

        make_blocks(steps, refs[2 * n :], make)

    return on_held(body, hidden + turned, block_shapes(steps, (hid // 2, quarter)), "out_blocks", me)


def ring_total(me, later, below0, above0, below1, above1, rowwise):
    block = later.shape[1:]
    if rowwise:
        cut = (2 * block[0] // SIDE, block[1])
    else:
        cut = (2 * block[0], block[1] // SIDE)

    def body(me_ref, later_ref, b0, a0, b1, a1, keep_ref, next_ref, prev_ref, far_ref, sum_ref):
        half = block[0]
        rows = half // SIDE

        def step(j):
            cut_j = span(j, rows)
            first = later_ref[2, cut_j].astype(F32) + b0[cut_j].astype(F32) + a0[1, cut_j].astype(F32)
            second = later_ref[3, cut_j].astype(F32) + b1[1, cut_j].astype(F32) + a1[cut_j].astype(F32)
            sum_ref[cut_j, :] = first
            sum_ref[span(j + SIDE, rows), :] = second

        repeat(SIDE, step, False)
        if rowwise:
            at = lax.rem(me_ref[0], SIDE)
        else:
            at = me_ref[0] // SIDE
        for k, ref in ((0, keep_ref), (1, next_ref), (3, prev_ref), (2, far_ref)):
            to = lax.rem(at + k, SIDE)
            if rowwise:
                v = sum_ref[pl.ds(pl.multiple_of(to * cut[0], cut[0]), cut[0]), :]
            else:
                v = sum_ref[:, pl.ds(pl.multiple_of(to * cut[1], cut[1]), cut[1])]
            ref[...] = v.astype(ref.dtype)

    return pl.pallas_call(
        body,
        in_specs=[IN_SMEM] + [IN_VMEM] * 5,
        out_specs=[IN_VMEM] * 4,
        out_shape=[pltpu.VMEM(cut, F32)] + [pltpu.VMEM(cut, BF16)] * 3,
        scratch_shapes=[pltpu.VMEM((2 * block[0], block[1]), F32)],
        compiler_params=params(12),
        cost_estimate=LITTLE,
        name="ring_total",
    )(me, *[held(a) for a in (later, below0, above0, below1, above1)])


def add_up(*groups):
    flat = [a for g in groups for a in g]

    def body(*refs):
        at = 0
        for g, out_ref in zip(groups, refs[len(flat) :]):
            total = refs[at][...].astype(F32)
            for ref in refs[at + 1 : at + len(g)]:
                total += ref[...].astype(F32)
            out_ref[...] = total
            at += len(g)

    return pl.pallas_call(
        body,
        in_specs=[IN_VMEM] * len(flat),
        out_specs=[IN_VMEM] * len(groups),
        out_shape=[jax.ShapeDtypeStruct(g[0].shape, F32) for g in groups],
        compiler_params=params(10),
        cost_estimate=LITTLE,
        name="add_up",
    )(*[held(a) for a in flat])


def after(values, *deps):
    return lax.optimization_barrier((values, deps))[0]


def on_device(tokens, picks, counts, score, w_in, w_out, cotan):
    routed = picks.shape[0]
    n_tok = tokens.shape[0]

    own_mine, me = take_rows(tokens, picks, counts, score, cotan)
    w_in, w_out = hold(*after((w_in, w_out), own_mine))
    near_mine = move_lane(own_mine, 1)
    own_other = swap_core(own_mine)
    own = hidden_units([[own_mine], [own_other]], w_in, w_out)

    near_other = move_lane(own_other, 1)
    near_mine = after(near_mine, own)
    far_mine = move_lane(near_mine, 1)
    swapped_mine = [swap_core(near_mine[:1]), swap_core(near_mine[1:])]
    own_terms = row_terms(own[0], own[1], w_in, w_out, routed, 1)
    own_got = swap_core(own_terms[1])
    near_mine, swapped_mine = after((near_mine, swapped_mine), own_terms)
    near = hidden_units([[near_mine], swapped_mine], w_in, w_out)
    near_terms = row_terms(near[0], near[1], w_in, w_out, routed, 3)

    near_other = after(near_other, near)
    swapped_other = [swap_core(near_other[:1]), swap_core(near_other[1:])]
    swapped_other, own_got = after((swapped_other, own_got), near_terms)
    other = hidden_units([[near_other], swapped_other], w_in, w_out, True)
    near_terms = row_terms(other[0], other[1], w_in, w_out, routed, 3, 1, near_terms)

    far_mine = after(far_mine, near_terms)
    far_packs = [far_mine, swap_core(far_mine)]
    far = hidden_units([[p] for p in far_packs], w_in, w_out, True)
    last_terms = row_terms(far[0], far[1], w_in, w_out, routed, 3, 2, near_terms, True)
    last_got = swap_core(last_terms[1])

    all_packs = [own_mine, own_other, near_mine, swapped_mine[0], near_other, swapped_other[0]] + far_packs
    hidden, dpre, turned = ([u[i] for u in (own, near, other, far)] for i in range(3))
    all_packs, dpre = after((all_packs, dpre), last_terms)
    in_up, in_down = in_blocks(me, all_packs, dpre, FIRST_STEP)
    in_below, in_above = move_x(in_up, 1), move_x(in_down, -1)

    hidden, turned = after((hidden, turned), in_up, in_down)
    out_up, out_down = out_blocks(me, hidden, turned, FIRST_STEP)
    out_below, out_above = move_y(out_up, 1), move_y(out_down, -1)

    last_got = after(last_got, out_up, out_down)
    to_far = (last_terms[0][2].astype(F32) + last_got[2].astype(F32)).astype(BF16)
    z_far = move_lane(to_far, -1)
    all_packs, dpre = after((all_packs, dpre), to_far)
    in_later = in_blocks(me, all_packs, dpre, LATER_STEP)[0]
    z_far = after(z_far, in_later)
    passed = jnp.pad(z_far.astype(F32)[None], ((0, 1), (0, 0), (0, 0), (0, 0)))
    to_near = (last_terms[0][:2].astype(F32) + last_got[:2].astype(F32) + passed).astype(BF16)
    z_near = move_lane(to_near, -1)
    hidden, turned = after((hidden, turned), to_near)
    out_later = out_blocks(me, hidden, turned, LATER_STEP)[0]

    def second_hop(later, from_below, from_above, move):
        up = (later[0].astype(F32) + from_below[0].astype(F32)).astype(BF16)
        down = (later[1].astype(F32) + from_above[0].astype(F32)).astype(BF16)
        return move(up, 1), move(down, -1), up, down

    in_below, in_above, out_below, out_above = after((in_below, in_above, out_below, out_above), out_later)
    in_hops = second_hop(in_later, in_below, in_above, move_x)
    out_hops = second_hop(out_later, out_below, out_above, move_y)
    in_total = ring_total(me, in_later, in_hops[0], in_above, in_below, in_hops[1], True)
    out_hops = after(out_hops[:2], in_total)
    z_near = after(z_near, in_total, out_hops)
    z_other = swap_core(z_near[1])

    def second_stage(total, move):
        keep, following, previous, far = total
        return keep, move(far, 2), move(following, 1), move(previous, -1)

    out_total = ring_total(me, out_later, out_hops[0], out_above, out_below, out_hops[1], False)
    in_total, out_total = after((in_total, out_total), z_other)
    in_parts = second_stage(in_total, move_y)
    out_parts = second_stage(out_total, move_x)

    back = (
        own_terms[0][0].astype(F32) + own_got[0].astype(F32) + z_near[0].astype(F32) + z_other.astype(F32)
    ).astype(BF16)
    ffn = back[0].astype(F32)
    heavy = (score[:, None] * ffn).astype(BF16)
    grad_score = jnp.sum(cotan.astype(F32) * ffn, axis=1)
    place = picks[:, None] == jnp.arange(n_tok, dtype=jnp.int32)[None, :]
    grad_x = dot(place.astype(BF16), back[1], ((0,), (0,))).astype(BF16)
    in_parts, out_parts = after((in_parts, out_parts), heavy, grad_x)
    grad_in, grad_out = add_up(in_parts, out_parts)
    return (heavy, grad_x, grad_score, grad_in, grad_out)


def solution(mesh):
    placed = (
        P(("ctx", "head"), None),
        P(("ctx", "head")),
        P(("ctx", "head")),
        P(("ctx", "head")),
        P(None, "head"),
        P("head", None),
        P(("ctx", "head"), None),
    )
    return jax.shard_map(
        on_device,
        mesh=mesh,
        in_specs=placed,
        out_specs=(
            P(("ctx", "head"), None),
            P(("ctx", "head"), None),
            P(("ctx", "head")),
            P("ctx", "head"),
            P("head", "ctx"),
        ),
        check_vma=False,
    )
```
